128 devices in a mesh: pool: 32 (over y, z, core), tp: 4 (over x).
Axes of the slice: x: 4, y: 4, z: 4, core: 2. Of those that a mesh axis runs over, the one named last changes fastest.
Arguments:
- queries: bfloat16 [96, 2, 8192], P('pool', None, 'tp'), may hold values from -6 to 6
- new_keys: bfloat16 [96, 2, 1024], P('pool', None, 'tp'), may hold values from -6 to 6
- new_values: bfloat16 [96, 2, 1024], P('pool', None, 'tp'), may hold values from -6 to 6
- home_keys: bfloat16 [96, 2048, 1024], P('pool', None, 'tp'), may hold values from -6 to 6
- home_values: bfloat16 [96, 2048, 1024], P('pool', None, 'tp'), may hold values from -6 to 6
- lent_keys: bfloat16 [384, 512, 1024], P('pool', None, 'tp'), may hold values from -6 to 6
- lent_values: bfloat16 [384, 512, 1024], P('pool', None, 'tp'), may hold values from -6 to 6
- lengths: int32 [96], replicated, may hold values from 1 to 4096, 196608 in all
- block_table: int32 [384], replicated, may hold values from 0 to 383, as said below
- out_weight: bfloat16 [8192, 8192], P('tp', 'pool'), may hold values from -0.0625 to 0.0625
Outputs:
- mixed: bfloat16 [96, 2, 8192], P('tp', None, 'pool')
The draws below stay inside these ranges and needn't reach their ends.
Inputs may be any that keep to these rules, and one draw needn't show every extreme that they name: `block_table`: A permutation: entry r * 4 + b is the global slot of request r's lent block b, and global slot g lies in the lent arrays' rows held by pool index g // 12; block b of request r is held by pool index (r // 3 + 1 + b * 5) mod 32, at a position among that index's 12 slots drawn from the seed; every slot is named once, also for blocks beyond a request's length. `lengths`: some request has exactly 4096 cached positions.
All inputs are finite; a program needn't handle non-finite values.
Results may differ from the reference program's by a relative error of at most 0.0055.
Values may be sent and summed in bfloat16 or wider, within the bound.
A program may use at most 64 MiB of HBM per device.

```python
import math
import jax
import jax.numpy as jnp
import numpy as np
from jax import lax

D = 8192
Q_HEADS = 64
KV_HEADS = 8
D_HEAD = 128
REQ_DEV = 3
HOME_LEN = 2048
BLOCK = 512
MAXB = 4
STEPS = 2
REQUESTS = 96
SLOTS = 12
MAXLEN = 4096
N_POOL = 32


def draw_home_keys(key, part):
    own_key = jax.random.fold_in(key, 11)
    shape = (REQUESTS, HOME_LEN, KV_HEADS * D_HEAD)
    return jax.random.truncated_normal(own_key, -6.0, 6.0, shape, jnp.float32).astype(jnp.bfloat16)


def draw_queries(key, part):
    own_key = jax.random.fold_in(key, 23)
    shape = (REQUESTS, STEPS, Q_HEADS * D_HEAD)
    return jax.random.truncated_normal(own_key, -6.0, 6.0, shape, jnp.float32).astype(jnp.bfloat16)


def draw_block_table(key, part):
    own_key = jax.random.fold_in(key, 37)
    lender_keys = jax.random.split(own_key, N_POOL)
    positions = jax.vmap(lambda one: jax.random.permutation(one, SLOTS))(lender_keys).astype(jnp.int32)
    request_ids = jnp.arange(REQUESTS, dtype=jnp.int32)
    homes = request_ids // REQ_DEV
    ranks = request_ids % REQ_DEV
    blocks = jnp.arange(MAXB, dtype=jnp.int32)
    reach = 1 + blocks * (N_POOL // 2 - 1) // (MAXB - 1)
    lenders = (homes[:, None] + reach[None, :]) % N_POOL
    within = blocks[None, :] * REQ_DEV + ranks[:, None]
    picked = positions[lenders, within]
    return (lenders * SLOTS + picked).reshape(REQUESTS * MAXB).astype(jnp.int32)


def block_levels(key, shape, cuts, least, largest):
    level, own = 1.0, jax.random.fold_in(key, 6)
    for dim, blocks in cuts:
        steps = jnp.exp(jax.random.uniform(jax.random.fold_in(own, dim), (blocks,), jnp.float32, least / len(cuts), largest / len(cuts)))
        level = level * jnp.repeat(steps, shape[dim] // blocks).reshape([-1 if axis == dim else 1 for axis in range(len(shape))])
    return level


def length_profile(count, total, most, skew):
    portions = [(1 << 20) // math.isqrt(rank ** skew) + 1 for rank in range(2, count + 1)]
    surplus, given = total - most - (count - 1), [1] * (count - 1)
    while surplus > 0:
        free = [i for i in range(count - 1) if given[i] < most]
        mass, budget = sum([portions[i] for i in free]), surplus
        for i in free:
            addition = min(most - given[i], max(1, budget * portions[i] // mass), surplus)
            given[i] = given[i] + addition
            surplus = surplus - addition
    return np.array([most] + given)


def ragged_sizes(rng, number_of, total, bound, slope):
    if number_of == 2:
        one = jax.random.randint(rng, (), max(1, total - bound), min(bound, total - 1) + 1)
        return jnp.stack([one, total - one])
    sizes = jnp.asarray(length_profile(number_of, total, bound, slope), jnp.int32)
    twos = (number_of - 1) // 2
    donor, receiver = sizes[1:1 + 2 * twos:2], sizes[2:2 + 2 * twos:2]
    slack = jnp.minimum(donor - 1, bound - receiver)
    passed = jax.random.randint(jax.random.fold_in(rng, 1), (twos,), 0, 1 << 20) % (slack + 1)
    sizes = sizes.at[1:1 + 2 * twos:2].set(donor - passed).at[2:2 + 2 * twos:2].set(receiver + passed)
    return sizes[jax.random.permutation(jax.random.fold_in(rng, 2), number_of)]


def bell_draw(stream_key, extent, spread, most, cuts=(), kind=jnp.bfloat16):
    result = jax.random.normal(stream_key, extent, jnp.float32) * spread
    if len(cuts) > 0:
        result = block_levels(stream_key, extent, cuts, -0.22, 0.18) * result
    return jnp.clip(result, min=-most, max=most).astype(kind)


def setup_inputs(seed: int = 0) -> dict:
    splits = jax.random.split(jax.random.key(seed), 11)
    queries = draw_queries(jax.random.fold_in(splits[10], 71), 0)
    new_keys = bell_draw(splits[1], (REQUESTS, STEPS, KV_HEADS * D_HEAD), 1.0, 6.0, ((0, 32), (2, 4)))
    new_values = bell_draw(splits[2], (REQUESTS, STEPS, KV_HEADS * D_HEAD), 1.0, 6.0, ((0, 32), (2, 4)))
    home_keys = draw_home_keys(jax.random.fold_in(splits[10], 71), 0)
    home_values = bell_draw(splits[4], (REQUESTS, HOME_LEN, KV_HEADS * D_HEAD), 1.0, 6.0, ((0, 32), (2, 4)))
    lent_keys = bell_draw(splits[5], (N_POOL * SLOTS, BLOCK, KV_HEADS * D_HEAD), 1.0, 6.0, ((0, 32), (2, 4)))
    lent_values = bell_draw(splits[6], (N_POOL * SLOTS, BLOCK, KV_HEADS * D_HEAD), 1.0, 6.0, ((0, 32), (2, 4)))
    lengths = ragged_sizes(splits[7], REQUESTS, REQUESTS * MAXLEN // 2, MAXLEN, 2).astype(jnp.int32)
    block_table = draw_block_table(jax.random.fold_in(splits[10], 71), 0)
    out_weight = bell_draw(splits[9], (Q_HEADS * D_HEAD, D), (Q_HEADS * D_HEAD) ** -0.5, 0.0625, ((0, 4), (1, 32)))
    return dict(queries=queries, new_keys=new_keys, new_values=new_values, home_keys=home_keys, home_values=home_values, lent_keys=lent_keys, lent_values=lent_values, lengths=lengths, block_table=block_table, out_weight=out_weight)


floor_score = -1.0e30


def reference(queries, new_keys, new_values, home_keys, home_values, lent_keys, lent_values, lengths, block_table, out_weight):
    factor = D_HEAD ** -0.5
    group_size = Q_HEADS // KV_HEADS
    span = MAXLEN + STEPS
    places = jnp.arange(span, dtype=jnp.int32)
    moments = jnp.arange(STEPS, dtype=jnp.int32)

    def per_request(request):
        entries = lax.dynamic_slice_in_dim(block_table, request * MAXB, MAXB)
        lent_k = jnp.take(lent_keys, entries, axis=0).reshape(MAXB * BLOCK, KV_HEADS * D_HEAD)
        lent_v = jnp.take(lent_values, entries, axis=0).reshape(MAXB * BLOCK, KV_HEADS * D_HEAD)
        keys_all = jnp.concatenate([home_keys[request], lent_k, new_keys[request]], axis=0)
        values_all = jnp.concatenate([home_values[request], lent_v, new_values[request]], axis=0)
        keys_all = keys_all.astype(jnp.float32).reshape(span, KV_HEADS, D_HEAD)
        values_all = values_all.astype(jnp.float32).reshape(span, KV_HEADS, D_HEAD)
        query = queries[request].astype(jnp.float32).reshape(STEPS, KV_HEADS, group_size, D_HEAD)
        scores = jnp.einsum("tgid,pgd->tgip", query, keys_all) * factor
        in_cache = places < lengths[request]
        fresh = (places[None, :] - MAXLEN) <= moments[:, None]
        visible = jnp.where(places[None, :] < MAXLEN, in_cache[None, :], fresh)
        scores = jnp.where(visible[:, None, None, :], scores, floor_score)
        peaks = jnp.max(scores, axis=-1, keepdims=True)
        weights = jnp.exp(scores - peaks)
        totals = jnp.sum(weights, axis=-1)
        rounded = lax.optimization_barrier(weights.astype(jnp.bfloat16)).astype(jnp.float32)
        summed = jnp.einsum("tgip,pgd->tgid", rounded, values_all)
        return (summed / totals[..., None]).reshape(STEPS, Q_HEADS * D_HEAD).astype(jnp.bfloat16)

    attended = lax.map(per_request, jnp.arange(REQUESTS, dtype=jnp.int32))
    mixed = jnp.dot(attended.reshape(REQUESTS * STEPS, Q_HEADS * D_HEAD), out_weight, preferred_element_type=jnp.float32)
    return mixed.reshape(REQUESTS, STEPS, D).astype(jnp.bfloat16)
```

```python
import functools
import math

import jax
import jax.numpy as jnp
from jax import lax
from jax.experimental import pallas as pl
from jax.experimental.pallas import tpu as pltpu
from jax.sharding import PartitionSpec as P

MESH = pl.DeviceIdType.MESH
F32, BF16 = jnp.float32, jnp.bfloat16

D_HEAD = 128
MAXB = 4
RANKS = 3
STEPS = 2
GROUP = 8
HEADS = 16
ROWS = STEPS * HEADS
HOME_LEN = 2048
BLOCK = 512
SLOTS = 12
POOL = 32
TP = 4
CHIPS = POOL // 2
PLANE = CHIPS // TP
KEPT = RANKS * STEPS * PLANE
FLOOR = -1e30
SCALE = math.log2(math.e) * D_HEAD**-0.5


def lender_of(pool, block):
    return lax.rem(pool + 1 + 5 * block, POOL)


def home_of(pool, block):
    return lax.rem(pool + POOL - 1 - 5 * block, POOL)


def gray(i):
    return i + i // 2 - 2 * (i // 3)


def by_head(left, right):
    parts = []
    for step in range(STEPS):
        at = step * HEADS
        parts += [left[at : at + GROUP], right[at + GROUP : at + HEADS]]
    return jnp.concatenate(parts, axis=0)


def spread(q):
    q = q.astype(F32)
    none = jnp.zeros_like(q)
    return jnp.concatenate([by_head(q, none), by_head(none, q)], axis=1).astype(BF16)


def scores_of(q_wide, keys, limit):
    scores = lax.dot_general(
        q_wide, keys, (((1,), (1,)), ((), ())), preferred_element_type=F32
    )
    places = lax.broadcasted_iota(jnp.int32, scores.shape, 1)
    return jnp.where(places < limit, scores, FLOOR)


def weigh(scores, peak, values):
    weights = jnp.exp2((scores - peak) * SCALE)
    total = jnp.sum(weights, axis=1, keepdims=True)
    summed = jnp.dot(weights.astype(BF16), values, preferred_element_type=F32)
    return total, by_head(summed[:, :D_HEAD], summed[:, D_HEAD:])


def kernel(
    q_hbm,
    nk_hbm,
    nv_hbm,
    hk_hbm,
    hv_hbm,
    lk_hbm,
    lv_hbm,
    len_hbm,
    table_hbm,
    w_hbm,
    out_ref,
    q_in,
    nk,
    nv,
    hk,
    hv,
    lk,
    lv,
    lengths,
    table,
    w,
    q_own,
    q_far,
    part,
    part_stats,
    back,
    back_stats,
    home_sum,
    home_peak,
    home_total,
    gathered,
    wide,
    left_side,
    sent,
    landed,
    small_sem,
    hk_sem,
    hv_sem,
    lent_sem,
    w_sem,
    q_send,
    q_recv,
    part_send,
    part_recv,
    stats_send,
    stats_recv,
    ag_send,
    ag_recv,
    rs_send,
    rs_recv,
):
    pool, tp = lax.axis_index("pool"), lax.axis_index("tp")
    core, chip = lax.rem(pool, 2), pool // 2
    y, z = chip // PLANE, lax.rem(chip, PLANE)
    sibling = chip * 2 + 1 - core

    small = [
        pltpu.make_async_copy(src, dst, small_sem.at[i])
        for i, (src, dst) in enumerate(
            [(q_hbm, q_in), (len_hbm, lengths), (table_hbm, table), (nk_hbm, nk), (nv_hbm, nv)]
        )
    ]
    for copy in small:
        copy.start()

    barrier = pltpu.get_barrier_semaphore()

    def tell(pool_to, tp_to):
        pl.semaphore_signal(barrier, inc=1, device_id=(pool_to, tp_to), device_id_type=MESH)

    for step in (1, 11, POOL - 1, POOL - 11):
        tell(lax.rem(pool + step, POOL), tp)
    for i in range(1, CHIPS):
        tell(lax.rem(chip + i, CHIPS) * 2 + core, tp)
    for i in range(1, TP):
        for half in range(2):
            tell(chip * 2 + half, lax.rem(tp + i, TP))

    def home_copies(r):
        return (
            pltpu.make_async_copy(hk_hbm.at[r], hk.at[r], hk_sem.at[r]),
            pltpu.make_async_copy(hv_hbm.at[r], hv.at[r], hv_sem.at[r]),
        )

    lent_copies = (
        pltpu.make_async_copy(lk_hbm, lk, lent_sem.at[0]),
        pltpu.make_async_copy(lv_hbm, lv, lent_sem.at[1]),
    )
    w_copy = pltpu.make_async_copy(w_hbm, w.at[core], w_sem.at[0])
    for copy in (*home_copies(0), *home_copies(1), *lent_copies, *home_copies(2)):
        copy.start()
    w_copy.start()

    small[0].wait()
    for r in range(RANKS):
        x = q_in[r].astype(F32)
        rows = [
            x[step : step + 1, head * D_HEAD : (head + 1) * D_HEAD]
            for step in range(STEPS)
            for head in range(HEADS)
        ]
        q_own[r] = jnp.concatenate(rows, axis=0).astype(BF16)

    pl.semaphore_wait(barrier, 4 + (CHIPS - 1) + 2 * (TP - 1))

    def q_copy(b):
        return pltpu.make_async_remote_copy(
            src_ref=q_own,
            dst_ref=q_far.at[b],
            send_sem=q_send.at[b],
            recv_sem=q_recv.at[b],
            device_id=(lender_of(pool, b), tp),
            device_id_type=MESH,
        )

    for b in range(MAXB):
        q_copy(b).start()
    w_over = pltpu.make_async_remote_copy(
        src_ref=w_hbm,
        dst_ref=w.at[core],
        send_sem=w_sem.at[1],
        recv_sem=w_sem.at[2],
        device_id=(sibling, tp),
        device_id_type=MESH,
    )
    w_over.start()

    for copy in small[1:]:
        copy.wait()

    def at_home(r):
        for copy in home_copies(r):
            copy.wait()
        q = q_own[r]
        scores = scores_of(spread(q), hk[r], lengths[pool * RANKS + r])
        peak = jnp.max(scores, axis=1, keepdims=True)
        q = q.astype(F32)
        new_k, new_v = nk[r].astype(F32), nv[r].astype(F32)
        steps = lax.broadcasted_iota(jnp.int32, (ROWS, 1), 0) // HEADS

        def of_new(x, j):
            shape = (ROWS, D_HEAD)
            left = jnp.broadcast_to(x[j : j + 1, :D_HEAD], shape)
            return by_head(left, jnp.broadcast_to(x[j : j + 1, D_HEAD:], shape))

        fresh = []
        for j in range(STEPS):
            score = jnp.sum(q * of_new(new_k, j), axis=1, keepdims=True)
            fresh.append(jnp.where(steps >= j, score, FLOOR))
            peak = jnp.maximum(peak, fresh[j])
        total, summed = weigh(scores, peak, hv[r])
        for j in range(STEPS):
            weight = jnp.exp2((fresh[j] - peak) * SCALE)
            total = total + weight
            summed = summed + weight.astype(BF16).astype(F32) * of_new(new_v, j)
        home_sum[r] = summed
        home_peak[r] = jnp.broadcast_to(peak, (ROWS, D_HEAD))
        home_total[r] = jnp.broadcast_to(total, (ROWS, D_HEAD))

    at_home(0)
    at_home(1)

    for copy in lent_copies:
        copy.wait()
    for b in range(MAXB):
        q_copy(b).wait_recv()

    eye = lax.broadcasted_iota(jnp.int32, (ROWS, D_HEAD), 0) == lax.broadcasted_iota(
        jnp.int32, (ROWS, D_HEAD), 1
    )

    def as_row(column):
        return jnp.sum(jnp.where(eye, column, 0.0), axis=0, keepdims=True)

    def as_column(row):
        return jnp.sum(jnp.where(eye, row, 0.0), axis=1, keepdims=True)

    def part_copies(b):
        home = (home_of(pool, b), tp)
        return (
            pltpu.make_async_remote_copy(
                src_ref=part.at[b],
                dst_ref=back.at[b],
                send_sem=part_send.at[b],
                recv_sem=part_recv.at[b],
                device_id=home,
                device_id_type=MESH,
            ),
            pltpu.make_async_remote_copy(
                src_ref=part_stats.at[b],
                dst_ref=back_stats.at[b],
                send_sem=stats_send.at[b],
                recv_sem=stats_recv.at[b],
                device_id=home,
                device_id_type=MESH,
            ),
        )

    def lend(b, carry):
        home = home_of(pool, b)
        stats = []
        for r in range(RANKS):
            request = home * RANKS + r
            slot = lax.rem(table[request * MAXB + b], SLOTS)
            limit = lengths[request] - HOME_LEN - b * BLOCK
            scores = scores_of(spread(q_far[b, r]), lk[slot], limit)
            peak = jnp.max(scores, axis=1, keepdims=True)
            total, summed = weigh(scores, peak, lv[slot])
            part[b, r] = summed.astype(BF16)
            stats += [as_row(peak), as_row(total)]
        stats.append(jnp.zeros((8 - len(stats), D_HEAD), F32))
        part_stats[b] = jnp.concatenate(stats, axis=0)
        for copy in part_copies(b):
            copy.start()
        return carry

    lax.fori_loop(0, MAXB, lend, 0)

    at_home(2)

    for b in range(MAXB):
        for copy in part_copies(b):
            copy.wait_recv()

    for r in range(RANKS):
        peaks, totals = [home_peak[r][:, :1]], [home_total[r][:, :1]]
        sums = [home_sum[r]]
        for b in range(MAXB):
            stats = back_stats[b]
            peaks.append(as_column(stats[2 * r : 2 * r + 1]))
            totals.append(as_column(stats[2 * r + 1 : 2 * r + 2]))
            sums.append(back[b, r].astype(F32))
        peak = functools.reduce(jnp.maximum, peaks)
        factors = [jnp.exp2((one - peak) * SCALE) for one in peaks]
        total = sum(f * one for f, one in zip(factors, totals))
        summed = sum(f * one for f, one in zip(factors, sums))
        gathered[chip, r * ROWS : (r + 1) * ROWS] = (summed / total).astype(BF16)

    def ag_copy(i):
        to_y = lax.rem(y + gray(i // PLANE), TP)
        to_z = lax.rem(z + gray(lax.rem(i, PLANE)), PLANE)
        return pltpu.make_async_remote_copy(
            src_ref=gathered.at[chip],
            dst_ref=gathered.at[chip],
            send_sem=ag_send.at[i],
            recv_sem=ag_recv.at[chip],
            device_id=((to_y * PLANE + to_z) * 2 + core, tp),
            device_id_type=MESH,
        )

    def ag_start(i, carry):
        ag_copy(i).start()
        return carry

    lax.fori_loop(1, CHIPS, ag_start, 0)

    w_copy.wait()
    w_over.wait_recv()

    def rs_copy(i, plane, half):
        return pltpu.make_async_remote_copy(
            src_ref=sent.at[i, half],
            dst_ref=landed.at[tp * 2 + core],
            send_sem=rs_send.at[i, half],
            recv_sem=rs_recv.at[tp * 2 + core],
            device_id=(chip * 2 + half, plane),
            device_id_type=MESH,
        )

    def ag_arrived(source):
        return pltpu.make_async_remote_copy(
            src_ref=gathered.at[source],
            dst_ref=gathered.at[source],
            send_sem=ag_send.at[0],
            recv_sem=ag_recv.at[source],
            device_id=(pool, tp),
            device_id_type=MESH,
        )

    def project(i, carry):
        plane = lax.rem(y + gray(i), TP)
        for each in range(PLANE):
            source = plane * PLANE + each

            @pl.when(source != chip)
            def _():
                ag_arrived(source).wait_recv()

            rows = RANKS * ROWS
            wide[each * rows : (each + 1) * rows] = gathered[source].astype(F32)
        for head in range(HEADS):
            left_side[:, head * D_HEAD : (head + 1) * D_HEAD] = wide[
                pl.ds(head, KEPT, stride=HEADS), :
            ].astype(BF16)
        lhs = left_side[...]
        for half in range(2):
            product = jnp.dot(lhs, w[half], preferred_element_type=F32)
            stacked = jnp.concatenate([product[:, :D_HEAD], product[:, D_HEAD:]], axis=0)
            stacked = stacked.astype(BF16)
            mine = jnp.logical_and(plane == tp, core == half)

            @pl.when(mine)
            def _():
                landed[tp * 2 + core] = stacked

            @pl.when(jnp.logical_not(mine))
            def _():
                sent[i, half] = stacked
                rs_copy(i, plane, half).start()

        return carry

    lax.fori_loop(0, TP, project, 0)

    def rs_arrived(source):
        return pltpu.make_async_remote_copy(
            src_ref=sent.at[0, 0],
            dst_ref=landed.at[source],
            send_sem=rs_send.at[0, 0],
            recv_sem=rs_recv.at[source],
            device_id=(pool, tp),
            device_id_type=MESH,
        )

    for source in range(TP * 2):

        @pl.when(source != tp * 2 + core)
        def _():
            rs_arrived(source).wait_recv()

    for half in range(2):
        both = landed[half].astype(F32)
        for i in range(1, TP):
            both = both + landed[i * 2 + half].astype(F32)
        both = jnp.concatenate([both[:KEPT], both[KEPT:]], axis=1)
        for each in range(PLANE):
            for r in range(RANKS):
                at = (each * RANKS + r) * STEPS
                out_ref[(each * 2 + half) * RANKS + r] = both[at : at + STEPS].astype(BF16)

    for b in range(MAXB):
        q_copy(b).wait_send()
        for copy in part_copies(b):
            copy.wait_send()
    w_over.wait_send()

    def ag_left(i, carry):
        ag_copy(i).wait_send()
        return carry

    lax.fori_loop(1, CHIPS, ag_left, 0)

    def rs_left(i, carry):
        plane = lax.rem(y + gray(i), TP)
        for half in range(2):

            @pl.when(jnp.logical_not(jnp.logical_and(plane == tp, core == half)))
            def _():
                rs_copy(i, plane, half).wait_send()

        return carry

    lax.fori_loop(0, TP, rs_left, 0)


def per_device(*args):
    dma = pltpu.SemaphoreType.DMA
    vmem = pltpu.VMEM
    scratch = [
        vmem((RANKS, STEPS, HEADS * D_HEAD), BF16),
        vmem((RANKS, STEPS, 2 * D_HEAD), BF16),
        vmem((RANKS, STEPS, 2 * D_HEAD), BF16),
        vmem((RANKS, HOME_LEN, 2 * D_HEAD), BF16),
        vmem((RANKS, HOME_LEN, 2 * D_HEAD), BF16),
        vmem((SLOTS, BLOCK, 2 * D_HEAD), BF16),
        vmem((SLOTS, BLOCK, 2 * D_HEAD), BF16),
        pltpu.SMEM((POOL * RANKS,), jnp.int32),
        pltpu.SMEM((POOL * RANKS * MAXB,), jnp.int32),
        vmem((2, HEADS * D_HEAD, 2 * D_HEAD), BF16),
        vmem((RANKS, ROWS, D_HEAD), BF16),
        vmem((MAXB, RANKS, ROWS, D_HEAD), BF16),
        vmem((MAXB, RANKS, ROWS, D_HEAD), BF16),
        vmem((MAXB, 8, D_HEAD), F32),
        vmem((MAXB, RANKS, ROWS, D_HEAD), BF16),
        vmem((MAXB, 8, D_HEAD), F32),
        vmem((RANKS, ROWS, D_HEAD), F32),
        vmem((RANKS, ROWS, D_HEAD), F32),
        vmem((RANKS, ROWS, D_HEAD), F32),
        vmem((CHIPS, RANKS * ROWS, D_HEAD), BF16),
        vmem((PLANE * RANKS * ROWS, D_HEAD), F32),
        vmem((KEPT, HEADS * D_HEAD), BF16),
        vmem((TP, 2, 2 * KEPT, D_HEAD), BF16),
        vmem((TP * 2, 2 * KEPT, D_HEAD), BF16),
        dma((5,)),
        dma((RANKS,)),
        dma((RANKS,)),
        dma((2,)),
        dma((3,)),
        dma((MAXB,)),
        dma((MAXB,)),
        dma((MAXB,)),
        dma((MAXB,)),
        dma((MAXB,)),
        dma((MAXB,)),
        dma((CHIPS,)),
        dma((CHIPS,)),
        dma((TP, 2)),
        dma((TP * 2,)),
    ]
    return pl.pallas_call(
        kernel,
        out_shape=jax.ShapeDtypeStruct((POOL * RANKS // TP, STEPS, 2 * D_HEAD), BF16),
        in_specs=[pl.BlockSpec(memory_space=pl.ANY)] * len(args),
        out_specs=pl.BlockSpec(memory_space=pltpu.VMEM),
        scratch_shapes=scratch,
        compiler_params=pltpu.CompilerParams(
            collective_id=0, has_side_effects=True, vmem_limit_bytes=48 * 2**20
        ),
    )(*args)


def solution(mesh):
    return jax.shard_map(
        per_device,
        mesh=mesh,
        in_specs=(
            P("pool", None, "tp"),
            P("pool", None, "tp"),
            P("pool", None, "tp"),
            P("pool", None, "tp"),
            P("pool", None, "tp"),
            P("pool", None, "tp"),
            P("pool", None, "tp"),
            P(),
            P(),
            P("tp", "pool"),
        ),
        out_specs=P("tp", None, "pool"),
        check_vma=False,
    )
```

```python
import functools
import math

import jax
import jax.numpy as jnp
from jax import lax
from jax.experimental import pallas as pl
from jax.experimental.pallas import tpu as pltpu
from jax.sharding import PartitionSpec as P

MESH = pl.DeviceIdType.MESH
F32, BF16 = jnp.float32, jnp.bfloat16

D_HEAD = 128
MAXB = 4
RANKS = 3
STEPS = 2
GROUP = 8
HEADS = 16
ROWS = STEPS * HEADS
HOME_LEN = 2048
BLOCK = 512
SLOTS = 12
POOL = 32
TP = 4
CHIPS = POOL // 2
PLANE = CHIPS // TP
KEPT = STEPS * PLANE
PART = ROWS + 16
FLOOR = -1e30
Q_ORDER = (2, 3, 1, 0)
GROUPS = ((0, 1), (2,))
FAR_FIRST = sorted(
    ((dy, dz) for dy in range(TP) for dz in range(PLANE)),
    key=lambda s: -sum(min(d, 4 - d) for d in s),
)
SCALE = math.log2(math.e) * D_HEAD**-0.5


def lender_of(pool, block):
    return lax.rem(pool + 1 + 5 * block, POOL)


def home_of(pool, block):
    return lax.rem(pool + POOL - 1 - 5 * block, POOL)


def by_head(left, right):
    parts = []
    for step in range(STEPS):
        at = step * HEADS
        parts += [left[at : at + GROUP], right[at + GROUP : at + HEADS]]
    return jnp.concatenate(parts, axis=0)


def spread(q):
    q = q.astype(F32)
    none = jnp.zeros_like(q)
    return jnp.concatenate([by_head(q, none), by_head(none, q)], axis=1).astype(BF16)


def scores_of(q_wide, keys, limit):
    scores = lax.dot_general(
        q_wide, keys, (((1,), (1,)), ((), ())), preferred_element_type=F32
    )
    places = lax.broadcasted_iota(jnp.int32, scores.shape, 1)
    return jnp.where(places < limit, scores, FLOOR)


def weigh(scores, peak, values):
    weights = jnp.exp2((scores - peak) * SCALE)
    total = jnp.sum(weights, axis=1, keepdims=True)
    summed = jnp.dot(weights.astype(BF16), values, preferred_element_type=F32)
    return total, by_head(summed[:, :D_HEAD], summed[:, D_HEAD:])


def kernel(
    q_hbm,
    nk_hbm,
    nv_hbm,
    hk_hbm,
    hv_hbm,
    lk_hbm,
    lv_hbm,
    len_hbm,
    table_hbm,
    w_hbm,
    out_ref,
    q_in,
    nk,
    nv,
    hk,
    hv,
    lk,
    lv,
    lengths,
    table,
    w,
    q_own,
    q_far,
    part,
    back,
    home_sum,
    home_peak,
    home_total,
    attended,
    gathered,
    wide,
    sent,
    landed,
    small_sem,
    hk_sem,
    hv_sem,
    lent_sem,
    w_sem,
    q_send,
    q_recv,
    part_send,
    part_recv,
    ag_send,
    ag_recv,
    rs_sem,
):
    pool, tp = lax.axis_index("pool"), lax.axis_index("tp")
    core, chip = lax.rem(pool, 2), pool // 2
    y, z = chip // PLANE, lax.rem(chip, PLANE)
    sibling = chip * 2 + 1 - core

    def remote(src, dst, send_sem, recv_sem, pool_to, tp_to):
        return pltpu.make_async_remote_copy(
            src_ref=src,
            dst_ref=dst,
            send_sem=send_sem,
            recv_sem=recv_sem,
            device_id=(pool_to, tp_to),
            device_id_type=MESH,
        )

    def wait_sent(ref, sem):
        remote(ref, ref, sem, sem, pool, tp).wait_send()

    def wait_come(ref, sem):
        remote(ref, ref, sem, sem, pool, tp).wait_recv()

    small = [
        pltpu.make_async_copy(src, dst, small_sem.at[i])
        for i, (src, dst) in enumerate(
            [(q_hbm, q_in), (len_hbm, lengths), (table_hbm, table), (nk_hbm, nk), (nv_hbm, nv)]
        )
    ]
    for copy in small:
        copy.start()

    barrier = pltpu.get_barrier_semaphore()

    def tell(pool_to, tp_to):
        pl.semaphore_signal(barrier, inc=1, device_id=(pool_to, tp_to), device_id_type=MESH)

    def chip_off(dy, dz):
        return lax.rem(y + dy, TP) * PLANE + lax.rem(z + dz, PLANE)

    for step in (16, 6, POOL - 6):
        tell(lax.rem(pool + step, POOL), tp)
    for dy, dz in FAR_FIRST:
        tell(chip_off(dy, dz) * 2 + 1 - core, tp)
    for i in (2, 1, 3):
        for half in range(2):
            tell(chip * 2 + half, lax.rem(tp + i, TP))

    def home_copies(r):
        return (
            pltpu.make_async_copy(hk_hbm.at[r], hk.at[r], hk_sem.at[r]),
            pltpu.make_async_copy(hv_hbm.at[r], hv.at[r], hv_sem.at[r]),
        )

    lent_copies = (
        pltpu.make_async_copy(lk_hbm, lk, lent_sem.at[0]),
        pltpu.make_async_copy(lv_hbm, lv, lent_sem.at[1]),
    )
    w_copy = pltpu.make_async_copy(w_hbm, w.at[core], w_sem.at[0])
    for copy in (*home_copies(0), *home_copies(1), *lent_copies, *home_copies(2), w_copy):
        copy.start()

    small[0].wait()
    for r in range(RANKS):
        x = q_in[r].astype(F32)
        rows = [
            x[step : step + 1, head * D_HEAD : (head + 1) * D_HEAD]
            for step in range(STEPS)
            for head in range(HEADS)
        ]
        q_own[r] = jnp.concatenate(rows, axis=0).astype(BF16)

    pl.semaphore_wait(barrier, 3 + CHIPS + 2 * (TP - 1))

    for r in range(RANKS):
        for b in Q_ORDER:
            to = lender_of(pool, b)
            remote(q_own.at[r], q_far.at[r, b], q_send, q_recv.at[r], to, tp).start()

    for copy in small[1:]:
        copy.wait()

    def at_home(r):
        for copy in home_copies(r):
            copy.wait()
        q = q_own[r]
        scores = scores_of(spread(q), hk[r], lengths[pool * RANKS + r])
        peak = jnp.max(scores, axis=1, keepdims=True)
        q = q.astype(F32)
        new_k, new_v = nk[r].astype(F32), nv[r].astype(F32)
        steps = lax.broadcasted_iota(jnp.int32, (ROWS, 1), 0) // HEADS

        def of_new(x, j):
            shape = (ROWS, D_HEAD)
            left = jnp.broadcast_to(x[j : j + 1, :D_HEAD], shape)
            return by_head(left, jnp.broadcast_to(x[j : j + 1, D_HEAD:], shape))

        fresh = []
        for j in range(STEPS):
            score = jnp.sum(q * of_new(new_k, j), axis=1, keepdims=True)
            fresh.append(jnp.where(steps >= j, score, FLOOR))
            peak = jnp.maximum(peak, fresh[j])
        total, summed = weigh(scores, peak, hv[r])
        for j in range(STEPS):
            weight = jnp.exp2((fresh[j] - peak) * SCALE)
            total = total + weight
            summed = summed + weight.astype(BF16).astype(F32) * of_new(new_v, j)
        home_sum[r] = summed
        home_peak[r] = jnp.broadcast_to(peak, (ROWS, D_HEAD))
        home_total[r] = jnp.broadcast_to(total, (ROWS, D_HEAD))

    at_home(0)
    at_home(1)

    for copy in lent_copies:
        copy.wait()

    eye = lax.broadcasted_iota(jnp.int32, (ROWS, D_HEAD), 0) == lax.broadcasted_iota(
        jnp.int32, (ROWS, D_HEAD), 1
    )

    def as_row(column):
        return jnp.sum(jnp.where(eye, column, 0.0), axis=0, keepdims=True)

    def as_column(row):
        return jnp.sum(jnp.where(eye, row, 0.0), axis=1, keepdims=True)

    def in_three(row):
        first = row.astype(BF16).astype(F32)
        second = (row - first).astype(BF16).astype(F32)
        return [first, second, row - first - second]

    def lent_slot(r, b):
        request = home_of(pool, b) * RANKS + r
        slot = lax.rem(table[request * MAXB + b], SLOTS)
        return slot, lengths[request] - HOME_LEN - b * BLOCK

    def lend(r):
        scores = []
        for b in range(MAXB):
            slot, limit = lent_slot(r, b)
            scores.append(scores_of(spread(q_far[r, b]), lk[slot], limit))
        for b in range(MAXB):
            slot, _ = lent_slot(r, b)
            peak = jnp.max(scores[b], axis=1, keepdims=True)
            total, summed = weigh(scores[b], peak, lv[slot])
            rows = [summed, *in_three(as_row(peak)), *in_three(as_row(total))]
            rows.append(jnp.zeros((PART - ROWS - 6, D_HEAD), F32))
            part[r, b] = jnp.concatenate(rows, axis=0).astype(BF16)
        for b in Q_ORDER:
            home = home_of(pool, b)
            remote(part.at[r, b], back.at[r, b], part_send, part_recv.at[r], home, tp).start()

    for r in range(RANKS):
        wait_come(q_far.at[r], q_recv.at[r])
        lend(r)

    w_over = remote(w_hbm, w.at[core], w_sem.at[1], w_sem.at[2], sibling, tp)
    w_over.start()
    at_home(2)

    def join(r):
        peaks, totals = [home_peak[r][:, :1]], [home_total[r][:, :1]]
        sums = [home_sum[r]]
        wait_come(back.at[r], part_recv.at[r])
        for b in range(MAXB):
            come = back[r, b].astype(F32)
            stats = come[ROWS:]
            sums.append(come[:ROWS])
            peaks.append(as_column(stats[0:1] + stats[1:2] + stats[2:3]))
            totals.append(as_column(stats[3:4] + stats[4:5] + stats[5:6]))
        peak = functools.reduce(jnp.maximum, peaks)
        factors = [jnp.exp2((one - peak) * SCALE) for one in peaks]
        total = sum(f * one for f, one in zip(factors, totals))
        summed = sum(f * one for f, one in zip(factors, sums))
        attended[r] = (summed / total).astype(BF16)
        for dy, dz in FAR_FIRST:
            to = chip_off(dy, dz) * 2 + 1 - core
            remote(attended.at[r], gathered.at[r, chip], ag_send.at[r], ag_recv.at[r], to, tp).start()

    for r in range(RANKS):
        join(r)

    w_copy.wait()
    w_over.wait_recv()

    theirs = tp * 2 + 1 - core

    def project(g):
        ranks = GROUPS[g]
        count = len(ranks)
        for r in ranks:
            wait_come(gathered.at[r], ag_recv.at[r])
        for k, r in enumerate(ranks):
            rows = CHIPS * ROWS
            wide[k * rows : (k + 1) * rows] = gathered[r].astype(F32).reshape(rows, D_HEAD)
        lhs = jnp.concatenate(
            [
                wide[pl.ds(head, count * CHIPS * STEPS, stride=HEADS), :].astype(BF16)
                for head in range(HEADS)
            ],
            axis=1,
        )
        first, size = ranks[0] * 2 * KEPT, count * 2 * KEPT
        there = landed.at[theirs, pl.ds(first, size)]
        for half in range(2):
            product = jnp.dot(lhs, w[half], preferred_element_type=F32)
            for plane in range(TP):
                rows = []
                for k in range(count):
                    at = k * CHIPS * STEPS + plane * KEPT
                    rows += [product[at : at + KEPT, :D_HEAD], product[at : at + KEPT, D_HEAD:]]
                sent[plane, half, first : first + size] = jnp.concatenate(rows, axis=0).astype(BF16)
            for i in (2, 1, 3):
                plane = lax.rem(tp + i, TP)
                here = sent.at[plane, half, pl.ds(first, size)]
                remote(here, there, rs_sem.at[0], rs_sem.at[1], chip * 2 + half, plane).start()
        here = sent.at[tp, 1 - core, pl.ds(first, size)]
        remote(here, there, rs_sem.at[0], rs_sem.at[1], sibling, tp).start()
        landed[theirs, first : first + size] = sent[tp, core, first : first + size]

    for g in range(len(GROUPS)):
        project(g)

    all_but_own = landed.at[pl.ds(0, 2 * TP - 1)]
    wait_come(all_but_own, rs_sem.at[1])
    for half in range(2):
        both = landed[half].astype(F32)
        for i in range(1, TP):
            both = both + landed[i * 2 + half].astype(F32)
        for r in range(RANKS):
            at = r * 2 * KEPT
            mine = [both[at : at + KEPT], both[at + KEPT : at + 2 * KEPT]]
            mine = jnp.concatenate(mine, axis=1).astype(BF16)
            for each in range(PLANE):
                at = each * STEPS
                out_ref[(each * 2 + half) * RANKS + r] = mine[at : at + STEPS]

    wait_sent(q_far, q_send)
    w_over.wait_send()
    wait_sent(part, part_send)
    for r in range(RANKS):
        wait_sent(gathered.at[r], ag_send.at[r])
    wait_sent(all_but_own, rs_sem.at[0])


def per_device(*args):
    dma = pltpu.SemaphoreType.DMA
    vmem = pltpu.VMEM
    scratch = [
        vmem((RANKS, STEPS, HEADS * D_HEAD), BF16),
        vmem((RANKS, STEPS, 2 * D_HEAD), BF16),
        vmem((RANKS, STEPS, 2 * D_HEAD), BF16),
        vmem((RANKS, HOME_LEN, 2 * D_HEAD), BF16),
        vmem((RANKS, HOME_LEN, 2 * D_HEAD), BF16),
        vmem((SLOTS, BLOCK, 2 * D_HEAD), BF16),
        vmem((SLOTS, BLOCK, 2 * D_HEAD), BF16),
        pltpu.SMEM((POOL * RANKS,), jnp.int32),
        pltpu.SMEM((POOL * RANKS * MAXB,), jnp.int32),
        vmem((2, HEADS * D_HEAD, 2 * D_HEAD), BF16),
        vmem((RANKS, ROWS, D_HEAD), BF16),
        vmem((RANKS, MAXB, ROWS, D_HEAD), BF16),
        vmem((RANKS, MAXB, PART, D_HEAD), BF16),
        vmem((RANKS, MAXB, PART, D_HEAD), BF16),
        vmem((RANKS, ROWS, D_HEAD), F32),
        vmem((RANKS, ROWS, D_HEAD), F32),
        vmem((RANKS, ROWS, D_HEAD), F32),
        vmem((RANKS, ROWS, D_HEAD), BF16),
        vmem((RANKS, CHIPS, ROWS, D_HEAD), BF16),
        vmem((RANKS * CHIPS * ROWS, D_HEAD), F32),
        vmem((TP, 2, RANKS * 2 * KEPT, D_HEAD), BF16),
        vmem((TP * 2, RANKS * 2 * KEPT, D_HEAD), BF16),
        dma((5,)),
        dma((RANKS,)),
        dma((RANKS,)),
        dma((2,)),
        dma((3,)),
        dma,
        dma((RANKS,)),
        dma,
        dma((RANKS,)),
        dma((RANKS,)),
        dma((RANKS,)),
        dma((2,)),
    ]
    return pl.pallas_call(
        kernel,
        out_shape=jax.ShapeDtypeStruct((POOL * RANKS // TP, STEPS, 2 * D_HEAD), BF16),
        in_specs=[pl.BlockSpec(memory_space=pl.ANY)] * len(args),
        out_specs=pl.BlockSpec(memory_space=pltpu.VMEM),
        scratch_shapes=scratch,
        compiler_params=pltpu.CompilerParams(
            collective_id=0, has_side_effects=True, vmem_limit_bytes=63 * 2**20
        ),
    )(*args)


def solution(mesh):
    return jax.shard_map(
        per_device,
        mesh=mesh,
        in_specs=(
            P("pool", None, "tp"),
            P("pool", None, "tp"),
            P("pool", None, "tp"),
            P("pool", None, "tp"),
            P("pool", None, "tp"),
            P("pool", None, "tp"),
            P("pool", None, "tp"),
            P(),
            P(),
            P("tp", "pool"),
        ),
        out_specs=P("tp", None, "pool"),
        check_vma=False,
    )
```

```python
import functools
import math

import jax
import jax.numpy as jnp
from jax import lax
from jax.experimental import pallas as pl
from jax.experimental.pallas import tpu as pltpu
from jax.sharding import PartitionSpec as P

MESH = pl.DeviceIdType.MESH
F32, BF16 = jnp.float32, jnp.bfloat16

D_HEAD = 128
MAXB = 4
RANKS = 3
STEPS = 2
GROUP = 8
HEADS = 16
ROWS = STEPS * HEADS
HOME_LEN = 2048
BLOCK = 512
SLOTS = 12
POOL = 32
TP = 4
CHIPS = POOL // 2
PLANE = CHIPS // TP
KEPT = STEPS * PLANE
PART = ROWS + 16
FLOOR = -1e30
Q_ORDER = (2, 3, 1, 0)
GROUPS = ((0, 1), (2,))
FAR_FIRST = sorted(
    ((dy, dz) for dy in range(TP) for dz in range(PLANE)),
    key=lambda s: -sum(min(d, 4 - d) for d in s),
)
SCALE = math.log2(math.e) * D_HEAD**-0.5


def lender_of(pool, block):
    return lax.rem(pool + 1 + 5 * block, POOL)


def home_of(pool, block):
    return lax.rem(pool + POOL - 1 - 5 * block, POOL)


def joiner_of(pool):
    return lax.rem(pool + 2 * PLANE, POOL)


def by_head(left, right):
    parts = []
    for step in range(STEPS):
        at = step * HEADS
        parts += [left[at : at + GROUP], right[at + GROUP : at + HEADS]]
    return jnp.concatenate(parts, axis=0)


def spread(q):
    q = q.astype(F32)
    none = jnp.zeros_like(q)
    return jnp.concatenate([by_head(q, none), by_head(none, q)], axis=1).astype(BF16)


def scores_of(q_wide, keys, limit):
    scores = lax.dot_general(
        q_wide, keys, (((1,), (1,)), ((), ())), preferred_element_type=F32
    )
    places = lax.broadcasted_iota(jnp.int32, scores.shape, 1)
    return jnp.where(places < limit, scores, FLOOR)


def weigh(scores, peak, values):
    weights = jnp.exp2((scores - peak) * SCALE)
    total = jnp.sum(weights, axis=1, keepdims=True)
    summed = jnp.dot(weights.astype(BF16), values, preferred_element_type=F32)
    return total, by_head(summed[:, :D_HEAD], summed[:, D_HEAD:])


def kernel(
    q_hbm,
    nk_hbm,
    nv_hbm,
    hk_hbm,
    hv_hbm,
    lk_hbm,
    lv_hbm,
    len_hbm,
    table_hbm,
    w_hbm,
    out_ref,
    q_in,
    nk,
    nv,
    hk,
    hv,
    lk,
    lv,
    lengths,
    table,
    w,
    q_own,
    q_far,
    home_part,
    home_back,
    part,
    back,
    attended,
    gathered,
    wide,
    sent,
    landed,
    small_sem,
    hk_sem,
    hv_sem,
    lent_sem,
    w_sem,
    q_send,
    q_recv,
    home_send,
    home_recv,
    part_send,
    part_recv,
    ag_send,
    ag_recv,
    rs_sem,
):
    pool, tp = lax.axis_index("pool"), lax.axis_index("tp")
    core, chip = lax.rem(pool, 2), pool // 2
    y, z = chip // PLANE, lax.rem(chip, PLANE)
    sibling = chip * 2 + 1 - core

    def remote(src, dst, send_sem, recv_sem, pool_to, tp_to):
        return pltpu.make_async_remote_copy(
            src_ref=src,
            dst_ref=dst,
            send_sem=send_sem,
            recv_sem=recv_sem,
            device_id=(pool_to, tp_to),
            device_id_type=MESH,
        )

    def wait_sent(ref, sem):
        remote(ref, ref, sem, sem, pool, tp).wait_send()

    def wait_come(ref, sem):
        remote(ref, ref, sem, sem, pool, tp).wait_recv()

    small = [
        pltpu.make_async_copy(src, dst, small_sem.at[i])
        for i, (src, dst) in enumerate(
            [(q_hbm, q_in), (len_hbm, lengths), (table_hbm, table), (nk_hbm, nk), (nv_hbm, nv)]
        )
    ]
    for copy in small:
        copy.start()

    barrier = pltpu.get_barrier_semaphore()

    def tell(pool_to, tp_to):
        pl.semaphore_signal(barrier, inc=1, device_id=(pool_to, tp_to), device_id_type=MESH)

    def chip_off(dy, dz):
        return lax.rem(y + dy, TP) * PLANE + lax.rem(z + dz, PLANE)

    for step in (-11, -16, -6, -7, -2, 3, 8, -8, 1, -1):
        tell(lax.rem(pool + POOL + step, POOL), tp)
    for i in (2, 1, 3):
        for half in range(2):
            tell(chip * 2 + half, lax.rem(tp + i, TP))

    def home_copies(r):
        return (
            pltpu.make_async_copy(hk_hbm.at[r], hk.at[r], hk_sem.at[r]),
            pltpu.make_async_copy(hv_hbm.at[r], hv.at[r], hv_sem.at[r]),
        )

    lent_copies = (
        pltpu.make_async_copy(lk_hbm, lk, lent_sem.at[0]),
        pltpu.make_async_copy(lv_hbm, lv, lent_sem.at[1]),
    )
    w_copy = pltpu.make_async_copy(w_hbm, w.at[core], w_sem.at[0])
    for copy in (*home_copies(0), *home_copies(1), *lent_copies, *home_copies(2), w_copy):
        copy.start()

    small[0].wait()
    for r in range(RANKS):
        x = q_in[r].astype(F32)
        rows = [
            x[step : step + 1, head * D_HEAD : (head + 1) * D_HEAD]
            for step in range(STEPS)
            for head in range(HEADS)
        ]
        q_own[r] = jnp.concatenate(rows, axis=0).astype(BF16)

    pl.semaphore_wait(barrier, 10 + 2 * (TP - 1))

    for r in range(RANKS):
        for b in Q_ORDER:
            to = lender_of(pool, b)
            remote(q_own.at[r], q_far.at[r, b], q_send, q_recv.at[r], to, tp).start()

    for copy in small[1:]:
        copy.wait()

    eye = lax.broadcasted_iota(jnp.int32, (ROWS, D_HEAD), 0) == lax.broadcasted_iota(
        jnp.int32, (ROWS, D_HEAD), 1
    )

    def as_row(column):
        return jnp.sum(jnp.where(eye, column, 0.0), axis=0, keepdims=True)

    def as_column(row):
        return jnp.sum(jnp.where(eye, row, 0.0), axis=1, keepdims=True)

    def in_three(row):
        first = row.astype(BF16).astype(F32)
        second = (row - first).astype(BF16).astype(F32)
        return [first, second, row - first - second]

    def message(summed, peak, total):
        rows = [summed, *in_three(as_row(peak)), *in_three(as_row(total))]
        rows.append(jnp.zeros((PART - ROWS - 6, D_HEAD), F32))
        return jnp.concatenate(rows, axis=0).astype(BF16)

    def left_over(summed):
        return (summed - summed.astype(BF16).astype(F32)).astype(BF16)

    def at_home(r):
        for copy in home_copies(r):
            copy.wait()
        q = q_own[r]
        scores = scores_of(spread(q), hk[r], lengths[pool * RANKS + r])
        peak = jnp.max(scores, axis=1, keepdims=True)
        q = q.astype(F32)
        new_k, new_v = nk[r].astype(F32), nv[r].astype(F32)
        steps = lax.broadcasted_iota(jnp.int32, (ROWS, 1), 0) // HEADS

        def of_new(x, j):
            shape = (ROWS, D_HEAD)
            left = jnp.broadcast_to(x[j : j + 1, :D_HEAD], shape)
            return by_head(left, jnp.broadcast_to(x[j : j + 1, D_HEAD:], shape))

        fresh = []
        for j in range(STEPS):
            score = jnp.sum(q * of_new(new_k, j), axis=1, keepdims=True)
            fresh.append(jnp.where(steps >= j, score, FLOOR))
            peak = jnp.maximum(peak, fresh[j])
        total, summed = weigh(scores, peak, hv[r])
        for j in range(STEPS):
            weight = jnp.exp2((fresh[j] - peak) * SCALE)
            total = total + weight
            summed = summed + weight.astype(BF16).astype(F32) * of_new(new_v, j)
        home_part[r, :PART] = message(summed, peak, total)
        home_part[r, PART:] = left_over(summed)
        there = home_back.at[r]
        remote(home_part.at[r], there, home_send, home_recv.at[r], joiner_of(pool), tp).start()

    for r in range(RANKS):
        at_home(r)

    for copy in lent_copies:
        copy.wait()

    def lent_slot(r, b):
        request = home_of(pool, b) * RANKS + r
        slot = lax.rem(table[request * MAXB + b], SLOTS)
        return slot, lengths[request] - HOME_LEN - b * BLOCK

    def lend(r):
        scores = []
        for b in range(MAXB):
            slot, limit = lent_slot(r, b)
            scores.append(scores_of(spread(q_far[r, b]), lk[slot], limit))
        for b in range(MAXB):
            slot, _ = lent_slot(r, b)
            peak = jnp.max(scores[b], axis=1, keepdims=True)
            total, summed = weigh(scores[b], peak, lv[slot])
            part[r, b] = message(summed, peak, total)
        for b in Q_ORDER:
            to = joiner_of(home_of(pool, b))
            remote(part.at[r, b], back.at[r, b], part_send, part_recv.at[r], to, tp).start()

    for r in range(RANKS):
        wait_come(q_far.at[r], q_recv.at[r])
        lend(r)

    w_over = remote(w_hbm, w.at[core], w_sem.at[1], w_sem.at[2], sibling, tp)
    w_over.start()
    def join(r):
        peaks, totals, sums = [], [], []
        wait_come(home_back.at[r], home_recv.at[r])
        wait_come(back.at[r], part_recv.at[r])
        for b in range(MAXB + 1):
            come = (back[r, b] if b < MAXB else home_back[r]).astype(F32)
            stats = come[ROWS:PART]
            sums.append(come[:ROWS] if b < MAXB else come[:ROWS] + come[PART:])
            peaks.append(as_column(stats[0:1] + stats[1:2] + stats[2:3]))
            totals.append(as_column(stats[3:4] + stats[4:5] + stats[5:6]))
        peak = functools.reduce(jnp.maximum, peaks)
        factors = [jnp.exp2((one - peak) * SCALE) for one in peaks]
        total = sum(f * one for f, one in zip(factors, totals))
        summed = sum(f * one for f, one in zip(factors, sums))
        attended[r] = (summed / total).astype(BF16)
        for dy, dz in FAR_FIRST:
            to = chip_off(dy, dz) * 2 + 1 - core
            remote(attended.at[r], gathered.at[r, chip], ag_send.at[r], ag_recv.at[r], to, tp).start()

    for r in range(RANKS):
        join(r)

    w_copy.wait()
    w_over.wait_recv()

    theirs = tp * 2 + 1 - core

    def joined_at(plane):
        return lax.rem(plane + 1, TP)

    def project(g):
        ranks = GROUPS[g]
        count = len(ranks)
        for r in ranks:
            wait_come(gathered.at[r], ag_recv.at[r])
        for k, r in enumerate(ranks):
            rows = CHIPS * ROWS
            wide[k * rows : (k + 1) * rows] = gathered[r].astype(F32).reshape(rows, D_HEAD)
        lhs = jnp.concatenate(
            [
                wide[pl.ds(head, count * CHIPS * STEPS, stride=HEADS), :].astype(BF16)
                for head in range(HEADS)
            ],
            axis=1,
        )
        first, size = ranks[0] * 2 * KEPT, count * 2 * KEPT
        there = landed.at[theirs, pl.ds(first, size)]
        for half in range(2):
            product = jnp.dot(lhs, w[half], preferred_element_type=F32)
            for plane in range(TP):
                rows = []
                for k in range(count):
                    at = k * CHIPS * STEPS + plane * KEPT
                    rows += [product[at : at + KEPT, :D_HEAD], product[at : at + KEPT, D_HEAD:]]
                sent[plane, half, first : first + size] = jnp.concatenate(rows, axis=0).astype(BF16)
            for i in (2, 1, 3):
                plane = lax.rem(tp + i, TP)
                here = sent.at[joined_at(plane), half, pl.ds(first, size)]
                remote(here, there, rs_sem.at[0], rs_sem.at[1], chip * 2 + half, plane).start()
        here = sent.at[joined_at(tp), 1 - core, pl.ds(first, size)]
        remote(here, there, rs_sem.at[0], rs_sem.at[1], sibling, tp).start()
        landed[theirs, first : first + size] = sent[joined_at(tp), core, first : first + size]

    for g in range(len(GROUPS)):
        project(g)

    all_but_own = landed.at[pl.ds(0, 2 * TP - 1)]
    wait_come(all_but_own, rs_sem.at[1])
    for half in range(2):
        both = landed[half].astype(F32)
        for i in range(1, TP):
            both = both + landed[i * 2 + half].astype(F32)
        for r in range(RANKS):
            at = r * 2 * KEPT
            mine = [both[at : at + KEPT], both[at + KEPT : at + 2 * KEPT]]
            mine = jnp.concatenate(mine, axis=1).astype(BF16)
            for each in range(PLANE):
                at = each * STEPS
                out_ref[(each * 2 + half) * RANKS + r] = mine[at : at + STEPS]

    wait_sent(q_far, q_send)
    w_over.wait_send()
    wait_sent(home_part, home_send)
    wait_sent(part, part_send)
    for r in range(RANKS):
        wait_sent(gathered.at[r], ag_send.at[r])
    wait_sent(all_but_own, rs_sem.at[0])


def per_device(*args):
    dma = pltpu.SemaphoreType.DMA
    vmem = pltpu.VMEM
    scratch = [
        vmem((RANKS, STEPS, HEADS * D_HEAD), BF16),
        vmem((RANKS, STEPS, 2 * D_HEAD), BF16),
        vmem((RANKS, STEPS, 2 * D_HEAD), BF16),
        vmem((RANKS, HOME_LEN, 2 * D_HEAD), BF16),
        vmem((RANKS, HOME_LEN, 2 * D_HEAD), BF16),
        vmem((SLOTS, BLOCK, 2 * D_HEAD), BF16),
        vmem((SLOTS, BLOCK, 2 * D_HEAD), BF16),
        pltpu.SMEM((POOL * RANKS,), jnp.int32),
        pltpu.SMEM((POOL * RANKS * MAXB,), jnp.int32),
        vmem((2, HEADS * D_HEAD, 2 * D_HEAD), BF16),
        vmem((RANKS, ROWS, D_HEAD), BF16),
        vmem((RANKS, MAXB, ROWS, D_HEAD), BF16),
        vmem((RANKS, PART + ROWS, D_HEAD), BF16),
        vmem((RANKS, PART + ROWS, D_HEAD), BF16),
        vmem((RANKS, MAXB, PART, D_HEAD), BF16),
        vmem((RANKS, MAXB, PART, D_HEAD), BF16),
        vmem((RANKS, ROWS, D_HEAD), BF16),
        vmem((RANKS, CHIPS, ROWS, D_HEAD), BF16),
        vmem((RANKS * CHIPS * ROWS, D_HEAD), F32),
        vmem((TP, 2, RANKS * 2 * KEPT, D_HEAD), BF16),
        vmem((TP * 2, RANKS * 2 * KEPT, D_HEAD), BF16),
        dma((5,)),
        dma((RANKS,)),
        dma((RANKS,)),
        dma((2,)),
        dma((3,)),
        dma,
        dma((RANKS,)),
        dma,
        dma((RANKS,)),
        dma,
        dma((RANKS,)),
        dma((RANKS,)),
        dma((RANKS,)),
        dma((2,)),
    ]
    return pl.pallas_call(
        kernel,
        out_shape=pltpu.VMEM((POOL * RANKS // TP, STEPS, 2 * D_HEAD), BF16),
        in_specs=[pl.BlockSpec(memory_space=pl.ANY)] * len(args),
        out_specs=pl.BlockSpec(memory_space=pltpu.VMEM),
        scratch_shapes=scratch,
        compiler_params=pltpu.CompilerParams(
            collective_id=0, has_side_effects=True, vmem_limit_bytes=60 * 2**20
        ),
    )(*args)


def solution(mesh):
    return jax.shard_map(
        per_device,
        mesh=mesh,
        in_specs=(
            P("pool", None, "tp"),
            P("pool", None, "tp"),
            P("pool", None, "tp"),
            P("pool", None, "tp"),
            P("pool", None, "tp"),
            P("pool", None, "tp"),
            P("pool", None, "tp"),
            P(),
            P(),
            P("tp", "pool"),
        ),
        out_specs=P("tp", None, "pool"),
        check_vma=False,
    )
```

```python
import functools
import math

import jax
import jax.numpy as jnp
from jax import lax
from jax.experimental import pallas as pl
from jax.experimental.pallas import tpu as pltpu
from jax.sharding import PartitionSpec as P

MESH = pl.DeviceIdType.MESH
F32, BF16 = jnp.float32, jnp.bfloat16

D_HEAD = 128
MAXB = 4
RANKS = 3
STEPS = 2
GROUP = 8
HEADS = 16
ROWS = STEPS * HEADS
HOME_LEN = 2048
BLOCK = 512
SLOTS = 12
POOL = 32
TP = 4
CHIPS = POOL // 2
PLANE = CHIPS // TP
KEPT = STEPS * PLANE
PART = ROWS + 16
FLOOR = -1e30
Q_ORDER = (2, 3, 1, 0)
GROUPS = ((0,), (1, 2))
FAR_FIRST = sorted(
    ((dy, dz) for dy in range(TP) for dz in range(PLANE)),
    key=lambda s: -sum(min(d, 4 - d) for d in s),
)
SCALE = math.log2(math.e) * D_HEAD**-0.5


def lender_of(pool, block):
    return lax.rem(pool + 1 + 5 * block, POOL)


def home_of(pool, block):
    return lax.rem(pool + POOL - 1 - 5 * block, POOL)


def joiner_of(pool):
    return lax.rem(pool + 2 * PLANE, POOL)


def by_head(left, right):
    parts = []
    for step in range(STEPS):
        at = step * HEADS
        parts += [left[at : at + GROUP], right[at + GROUP : at + HEADS]]
    return jnp.concatenate(parts, axis=0)


def spread(q):
    q = q.astype(F32)
    none = jnp.zeros_like(q)
    return jnp.concatenate([by_head(q, none), by_head(none, q)], axis=1).astype(BF16)


def scores_of(q_wide, keys, limit):
    scores = lax.dot_general(
        q_wide, keys, (((1,), (1,)), ((), ())), preferred_element_type=F32
    )
    places = lax.broadcasted_iota(jnp.int32, scores.shape, 1)
    return jnp.where(places < limit, scores, FLOOR)


def weigh(scores, peak, values):
    weights = jnp.exp2((scores - peak) * SCALE)
    total = jnp.sum(weights, axis=1, keepdims=True)
    summed = jnp.dot(weights.astype(BF16), values, preferred_element_type=F32)
    return total, by_head(summed[:, :D_HEAD], summed[:, D_HEAD:])


def kernel(
    q_hbm,
    nk_hbm,
    nv_hbm,
    hk_hbm,
    hv_hbm,
    lk_hbm,
    lv_hbm,
    len_hbm,
    table_hbm,
    w_hbm,
    out_ref,
    q_in,
    nk,
    nv,
    hk,
    hv,
    lk,
    lv,
    lengths,
    table,
    w,
    q_own,
    q_far,
    home_part,
    home_back,
    part,
    back,
    attended,
    gathered,
    wide,
    sent,
    landed,
    small_sem,
    hk_sem,
    hv_sem,
    lent_sem,
    w_sem,
    q_send,
    q_recv,
    home_send,
    home_recv,
    part_send,
    part_recv,
    ag_send,
    ag_recv,
    rs_sem,
):
    pool, tp = lax.axis_index("pool"), lax.axis_index("tp")
    core, chip = lax.rem(pool, 2), pool // 2
    y, z = chip // PLANE, lax.rem(chip, PLANE)
    sibling = chip * 2 + 1 - core

    def remote(src, dst, send_sem, recv_sem, pool_to, tp_to):
        return pltpu.make_async_remote_copy(
            src_ref=src,
            dst_ref=dst,
            send_sem=send_sem,
            recv_sem=recv_sem,
            device_id=(pool_to, tp_to),
            device_id_type=MESH,
        )

    def wait_sent(ref, sem):
        remote(ref, ref, sem, sem, pool, tp).wait_send()

    def wait_come(ref, sem):
        remote(ref, ref, sem, sem, pool, tp).wait_recv()

    barrier = pltpu.get_barrier_semaphore()

    def tell(pool_to, tp_to):
        pl.semaphore_signal(barrier, inc=1, device_id=(pool_to, tp_to), device_id_type=MESH)

    def chip_off(dy, dz):
        return lax.rem(y + dy, TP) * PLANE + lax.rem(z + dz, PLANE)

    for step in (-16, -6, -11, -7, -2, 3, 8, -8, 1, -1):
        tell(lax.rem(pool + POOL + step, POOL), tp)
    for i in (2, 1, 3):
        for half in range(2):
            tell(chip * 2 + half, lax.rem(tp + i, TP))

    small = [
        pltpu.make_async_copy(src, dst, small_sem.at[i])
        for i, (src, dst) in enumerate(
            [(q_hbm, q_in), (len_hbm, lengths), (table_hbm, table), (nk_hbm, nk), (nv_hbm, nv)]
        )
    ]
    for copy in small:
        copy.start()

    def home_copies(r):
        return (
            pltpu.make_async_copy(hk_hbm.at[r], hk.at[r], hk_sem.at[r]),
            pltpu.make_async_copy(hv_hbm.at[r], hv.at[r], hv_sem.at[r]),
        )

    lent_copies = (
        pltpu.make_async_copy(lk_hbm, lk, lent_sem.at[0]),
        pltpu.make_async_copy(lv_hbm, lv, lent_sem.at[1]),
    )
    w_copy = pltpu.make_async_copy(w_hbm, w.at[core], w_sem.at[0])
    for copy in (*home_copies(0), *home_copies(1), *lent_copies, *home_copies(2), w_copy):
        copy.start()

    small[0].wait()
    for r in range(RANKS):
        x = q_in[r].astype(F32)
        rows = [
            x[step : step + 1, head * D_HEAD : (head + 1) * D_HEAD]
            for step in range(STEPS)
            for head in range(HEADS)
        ]
        q_own[r] = jnp.concatenate(rows, axis=0).astype(BF16)

    pl.semaphore_wait(barrier, 10 + 2 * (TP - 1))

    for r in range(RANKS):
        for b in Q_ORDER:
            to = lender_of(pool, b)
            remote(q_own.at[r], q_far.at[r, b], q_send, q_recv.at[r], to, tp).start()

    for copy in small[1:]:
        copy.wait()

    eye = lax.broadcasted_iota(jnp.int32, (ROWS, D_HEAD), 0) == lax.broadcasted_iota(
        jnp.int32, (ROWS, D_HEAD), 1
    )

    def as_row(column):
        return jnp.sum(jnp.where(eye, column, 0.0), axis=0, keepdims=True)

    def as_column(row):
        return jnp.sum(jnp.where(eye, row, 0.0), axis=1, keepdims=True)

    def in_three(row):
        first = row.astype(BF16).astype(F32)
        second = (row - first).astype(BF16).astype(F32)
        return [first, second, row - first - second]

    def message(summed, peak, total):
        rows = [summed, *in_three(as_row(peak)), *in_three(as_row(total))]
        rows.append(jnp.zeros((PART - ROWS - 6, D_HEAD), F32))
        return jnp.concatenate(rows, axis=0).astype(BF16)

    def left_over(summed):
        return (summed - summed.astype(BF16).astype(F32)).astype(BF16)

    def at_home(r):
        for copy in home_copies(r):
            copy.wait()
        q = q_own[r]
        scores = scores_of(spread(q), hk[r], lengths[pool * RANKS + r])
        peak = jnp.max(scores, axis=1, keepdims=True)
        q = q.astype(F32)
        new_k, new_v = nk[r].astype(F32), nv[r].astype(F32)
        steps = lax.broadcasted_iota(jnp.int32, (ROWS, 1), 0) // HEADS

        def of_new(x, j):
            shape = (ROWS, D_HEAD)
            left = jnp.broadcast_to(x[j : j + 1, :D_HEAD], shape)
            return by_head(left, jnp.broadcast_to(x[j : j + 1, D_HEAD:], shape))

        fresh = []
        for j in range(STEPS):
            score = jnp.sum(q * of_new(new_k, j), axis=1, keepdims=True)
            fresh.append(jnp.where(steps >= j, score, FLOOR))
            peak = jnp.maximum(peak, fresh[j])
        total, summed = weigh(scores, peak, hv[r])
        for j in range(STEPS):
            weight = jnp.exp2((fresh[j] - peak) * SCALE)
            total = total + weight
            summed = summed + weight.astype(BF16).astype(F32) * of_new(new_v, j)
        home_part[r, :PART] = message(summed, peak, total)
        home_part[r, PART:] = left_over(summed)
        there = home_back.at[r]
        remote(home_part.at[r], there, home_send, home_recv.at[r], joiner_of(pool), tp).start()

    for r in range(RANKS):
        at_home(r)

    for copy in lent_copies:
        copy.wait()

    def lent_slot(r, b):
        request = home_of(pool, b) * RANKS + r
        slot = lax.rem(table[request * MAXB + b], SLOTS)
        return slot, lengths[request] - HOME_LEN - b * BLOCK

    def lend(r):
        scores = []
        for b in range(MAXB):
            slot, limit = lent_slot(r, b)
            scores.append(scores_of(spread(q_far[r, b]), lk[slot], limit))
        for b in range(MAXB):
            slot, _ = lent_slot(r, b)
            peak = jnp.max(scores[b], axis=1, keepdims=True)
            total, summed = weigh(scores[b], peak, lv[slot])
            part[r, b] = message(summed, peak, total)
        for b in Q_ORDER:
            to = joiner_of(home_of(pool, b))
            remote(part.at[r, b], back.at[r, b], part_send, part_recv.at[r], to, tp).start()

    for r in range(RANKS):
        wait_come(q_far.at[r], q_recv.at[r])
        lend(r)

    w_over = remote(w_hbm, w.at[core], w_sem.at[1], w_sem.at[2], sibling, tp)
    w_over.start()
    def join(r):
        peaks, totals, sums = [], [], []
        wait_come(home_back.at[r], home_recv.at[r])
        wait_come(back.at[r], part_recv.at[r])
        for b in range(MAXB + 1):
            come = (back[r, b] if b < MAXB else home_back[r]).astype(F32)
            stats = come[ROWS:PART]
            sums.append(come[:ROWS] if b < MAXB else come[:ROWS] + come[PART:])
            peaks.append(as_column(stats[0:1] + stats[1:2] + stats[2:3]))
            totals.append(as_column(stats[3:4] + stats[4:5] + stats[5:6]))
        peak = functools.reduce(jnp.maximum, peaks)
        factors = [jnp.exp2((one - peak) * SCALE) for one in peaks]
        total = sum(f * one for f, one in zip(factors, totals))
        summed = sum(f * one for f, one in zip(factors, sums))
        attended[r] = (summed / total).astype(BF16)

    def spread_out(ranks):
        first, count = ranks[0], len(ranks)
        mine = attended.at[pl.ds(first, count)]
        there = gathered.at[chip, pl.ds(first, count)]

        def give(to):
            to = to * 2 + 1 - core
            remote(mine, there, ag_send.at[first], ag_recv.at[first], to, tp).start()

        give(0)
        for dy, dz in FAR_FIRST:
            to = chip_off(dy, dz)
            pl.when(to != 0)(functools.partial(give, to))

    for ranks in GROUPS:
        for r in ranks:
            join(r)
        spread_out(ranks)

    w_copy.wait()
    w_over.wait_recv()

    theirs = tp * 2 + 1 - core

    def joined_at(plane):
        return lax.rem(plane + 1, TP)

    def project(g):
        ranks = GROUPS[g]
        count = len(ranks)
        come = gathered.at[:, pl.ds(ranks[0], count)]
        wait_come(come, ag_recv.at[ranks[0]])
        for k, r in enumerate(ranks):
            rows = CHIPS * ROWS
            wide[k * rows : (k + 1) * rows] = gathered[:, r].astype(F32).reshape(rows, D_HEAD)
        lhs = jnp.concatenate(
            [
                wide[pl.ds(head, count * CHIPS * STEPS, stride=HEADS), :].astype(BF16)
                for head in range(HEADS)
            ],
            axis=1,
        )
        first, size = ranks[0] * 2 * KEPT, count * 2 * KEPT
        there = landed.at[theirs, pl.ds(first, size)]
        for half in (1, 0):
            product = jnp.dot(lhs, w[half], preferred_element_type=F32)
            for plane in range(TP):
                rows = []
                for k in range(count):
                    at = k * CHIPS * STEPS + plane * KEPT
                    rows += [product[at : at + KEPT, :D_HEAD], product[at : at + KEPT, D_HEAD:]]
                sent[plane, half, first : first + size] = jnp.concatenate(rows, axis=0).astype(BF16)
            for i in (2, 1, 3):
                plane = lax.rem(tp + i, TP)
                here = sent.at[joined_at(plane), half, pl.ds(first, size)]
                remote(here, there, rs_sem.at[0], rs_sem.at[1], chip * 2 + half, plane).start()
        here = sent.at[joined_at(tp), 1 - core, pl.ds(first, size)]
        remote(here, there, rs_sem.at[0], rs_sem.at[1], sibling, tp).start()
        landed[theirs, first : first + size] = sent[joined_at(tp), core, first : first + size]

    for g in range(len(GROUPS)):
        project(g)

    all_but_own = landed.at[pl.ds(0, 2 * TP - 1)]
    wait_come(all_but_own, rs_sem.at[1])
    for half in range(2):
        both = landed[half].astype(F32)
        for i in range(1, TP):
            both = both + landed[i * 2 + half].astype(F32)
        for r in range(RANKS):
            at = r * 2 * KEPT
            mine = [both[at : at + KEPT], both[at + KEPT : at + 2 * KEPT]]
            mine = jnp.concatenate(mine, axis=1).astype(BF16)
            for each in range(PLANE):
                at = each * STEPS
                out_ref[(each * 2 + half) * RANKS + r] = mine[at : at + STEPS]

    wait_sent(q_far, q_send)
    w_over.wait_send()
    wait_sent(home_part, home_send)
    wait_sent(part, part_send)
    for ranks in GROUPS:
        gone = gathered.at[:, pl.ds(ranks[0], len(ranks))]
        wait_sent(gone, ag_send.at[ranks[0]])
    wait_sent(all_but_own, rs_sem.at[0])


def per_device(*args):
    dma = pltpu.SemaphoreType.DMA
    vmem = pltpu.VMEM
    scratch = [
        vmem((RANKS, STEPS, HEADS * D_HEAD), BF16),
        vmem((RANKS, STEPS, 2 * D_HEAD), BF16),
        vmem((RANKS, STEPS, 2 * D_HEAD), BF16),
        vmem((RANKS, HOME_LEN, 2 * D_HEAD), BF16),
        vmem((RANKS, HOME_LEN, 2 * D_HEAD), BF16),
        vmem((SLOTS, BLOCK, 2 * D_HEAD), BF16),
        vmem((SLOTS, BLOCK, 2 * D_HEAD), BF16),
        pltpu.SMEM((POOL * RANKS,), jnp.int32),
        pltpu.SMEM((POOL * RANKS * MAXB,), jnp.int32),
        vmem((2, HEADS * D_HEAD, 2 * D_HEAD), BF16),
        vmem((RANKS, ROWS, D_HEAD), BF16),
        vmem((RANKS, MAXB, ROWS, D_HEAD), BF16),
        vmem((RANKS, PART + ROWS, D_HEAD), BF16),
        vmem((RANKS, PART + ROWS, D_HEAD), BF16),
        vmem((RANKS, MAXB, PART, D_HEAD), BF16),
        vmem((RANKS, MAXB, PART, D_HEAD), BF16),
        vmem((RANKS, ROWS, D_HEAD), BF16),
        vmem((CHIPS, RANKS, ROWS, D_HEAD), BF16),
        vmem((RANKS * CHIPS * ROWS, D_HEAD), F32),
        vmem((TP, 2, RANKS * 2 * KEPT, D_HEAD), BF16),
        vmem((TP * 2, RANKS * 2 * KEPT, D_HEAD), BF16),
        dma((5,)),
        dma((RANKS,)),
        dma((RANKS,)),
        dma((2,)),
        dma((3,)),
        dma,
        dma((RANKS,)),
        dma,
        dma((RANKS,)),
        dma,
        dma((RANKS,)),
        dma((RANKS,)),
        dma((RANKS,)),
        dma((2,)),
    ]
    return pl.pallas_call(
        kernel,
        out_shape=pltpu.VMEM((POOL * RANKS // TP, STEPS, 2 * D_HEAD), BF16),
        in_specs=[pl.BlockSpec(memory_space=pl.ANY)] * len(args),
        out_specs=pl.BlockSpec(memory_space=pltpu.VMEM),
        scratch_shapes=scratch,
        compiler_params=pltpu.CompilerParams(
            collective_id=0, has_side_effects=True, vmem_limit_bytes=60 * 2**20
        ),
    )(*args)


def solution(mesh):
    return jax.shard_map(
        per_device,
        mesh=mesh,
        in_specs=(
            P("pool", None, "tp"),
            P("pool", None, "tp"),
            P("pool", None, "tp"),
            P("pool", None, "tp"),
            P("pool", None, "tp"),
            P("pool", None, "tp"),
            P("pool", None, "tp"),
            P(),
            P(),
            P("tp", "pool"),
        ),
        out_specs=P("tp", None, "pool"),
        check_vma=False,
    )
```

```python
import functools
import math

import jax
import jax.numpy as jnp
from jax import lax
from jax.experimental import pallas as pl
from jax.experimental.pallas import tpu as pltpu
from jax.sharding import PartitionSpec as P

MESH = pl.DeviceIdType.MESH
F32, BF16 = jnp.float32, jnp.bfloat16

D_HEAD = 128
MAXB = 4
RANKS = 3
STEPS = 2
GROUP = 8
HEADS = 16
ROWS = STEPS * HEADS
HOME_LEN = 2048
BLOCK = 512
SLOTS = 12
POOL = 32
TP = 4
CHIPS = POOL // 2
PLANE = CHIPS // TP
KEPT = STEPS * PLANE
PART = ROWS + 16
HOME_AT = MAXB * PART
FLOOR = -1e30
Q_ORDER = (2, 3, 1, 0)
GROUPS = ((0,), (1, 2))
FAR_FIRST = sorted(
    ((dy, dz) for dy in range(TP) for dz in range(PLANE)),
    key=lambda s: -sum(min(d, 4 - d) for d in s),
)
SCALE = math.log2(math.e) * D_HEAD**-0.5


def lender_of(pool, block):
    return lax.rem(pool + 1 + 5 * block, POOL)


def home_of(pool, block):
    return lax.rem(pool + POOL - 1 - 5 * block, POOL)


def joiner_of(pool):
    return lax.rem(pool + 2 * PLANE, POOL)


def by_head(left, right):
    parts = []
    for step in range(STEPS):
        at = step * HEADS
        parts += [left[at : at + GROUP], right[at + GROUP : at + HEADS]]
    return jnp.concatenate(parts, axis=0)


def spread(q):
    q = q.astype(F32)
    none = jnp.zeros_like(q)
    return jnp.concatenate([by_head(q, none), by_head(none, q)], axis=1).astype(BF16)


def scores_of(q_wide, keys, limit):
    scores = lax.dot_general(
        q_wide, keys, (((1,), (1,)), ((), ())), preferred_element_type=F32
    )
    places = lax.broadcasted_iota(jnp.int32, scores.shape, 1)
    return jnp.where(places < limit, scores, FLOOR)


def weigh(scores, peak, values):
    weights = jnp.exp2((scores - peak) * SCALE)
    total = jnp.sum(weights, axis=1, keepdims=True)
    summed = jnp.dot(weights.astype(BF16), values, preferred_element_type=F32)
    return total, by_head(summed[:, :D_HEAD], summed[:, D_HEAD:])


def kernel(
    q_hbm,
    nk_hbm,
    nv_hbm,
    hk_hbm,
    hv_hbm,
    lk_hbm,
    lv_hbm,
    len_hbm,
    table_hbm,
    w_hbm,
    out_ref,
    q_in,
    nk,
    nv,
    home_kv,
    lent_kv,
    lengths,
    table,
    w,
    q_own,
    q_far,
    part,
    back,
    attended,
    gathered,
    wide,
    sent,
    landed,
    small_sem,
    home_sem,
    lent_sem,
    w_sem,
    q_send,
    q_recv,
    part_send,
    part_recv,
    ag_send,
    ag_recv,
    rs_sem,
):
    pool, tp = lax.axis_index("pool"), lax.axis_index("tp")
    core, chip = lax.rem(pool, 2), pool // 2
    y, z = chip // PLANE, lax.rem(chip, PLANE)
    sibling = chip * 2 + 1 - core

    def remote(src, dst, send_sem, recv_sem, pool_to, tp_to):
        return pltpu.make_async_remote_copy(
            src_ref=src,
            dst_ref=dst,
            send_sem=send_sem,
            recv_sem=recv_sem,
            device_id=(pool_to, tp_to),
            device_id_type=MESH,
        )

    def wait_sent(ref, sem):
        remote(ref, ref, sem, sem, pool, tp).wait_send()

    def wait_come(ref, sem):
        remote(ref, ref, sem, sem, pool, tp).wait_recv()

    def wait_here(ref, sem):
        pltpu.make_async_copy(ref, ref, sem).wait()

    barrier = pltpu.get_barrier_semaphore()

    def tell(pool_to, tp_to):
        pl.semaphore_signal(barrier, inc=1, device_id=(pool_to, tp_to), device_id_type=MESH)

    def chip_off(dy, dz):
        return lax.rem(y + dy, TP) * PLANE + lax.rem(z + dz, PLANE)

    for step in (-16, -6, -11, -1):
        tell(lax.rem(pool + POOL + step, POOL), tp)

    small = [
        pltpu.make_async_copy(src, dst, small_sem.at[i])
        for i, (src, dst) in enumerate(
            [(q_hbm, q_in), (len_hbm, lengths), (table_hbm, table), (nk_hbm, nk), (nv_hbm, nv)]
        )
    ]
    for copy in small:
        copy.start()

    for step in (-7, -2, 3, 8, -8, 1):
        tell(lax.rem(pool + POOL + step, POOL), tp)
    for i in (2, 1, 3):
        for half in range(2):
            tell(chip * 2 + half, lax.rem(tp + i, TP))

    def home_copies(r):
        return (
            pltpu.make_async_copy(hk_hbm.at[r], home_kv.at[0, r], home_sem.at[r]),
            pltpu.make_async_copy(hv_hbm.at[r], home_kv.at[1, r], home_sem.at[r]),
        )

    lent_copies = (
        pltpu.make_async_copy(lk_hbm, lent_kv.at[0], lent_sem),
        pltpu.make_async_copy(lv_hbm, lent_kv.at[1], lent_sem),
    )
    w_copy = pltpu.make_async_copy(w_hbm, w.at[core], w_sem.at[0])
    for copy in (*home_copies(0), *home_copies(1), *lent_copies, *home_copies(2), w_copy):
        copy.start()

    small[0].wait()
    for r in range(RANKS):
        x = q_in[r].astype(F32)
        rows = [
            x[step : step + 1, head * D_HEAD : (head + 1) * D_HEAD]
            for step in range(STEPS)
            for head in range(HEADS)
        ]
        q_own[r] = jnp.concatenate(rows, axis=0).astype(BF16)

    pl.semaphore_wait(barrier, 10 + 2 * (TP - 1))

    for r in range(RANKS):
        for b in Q_ORDER:
            to = lender_of(pool, b)
            remote(q_own.at[r], q_far.at[r, b], q_send, q_recv.at[r], to, tp).start()

    for copy in small[1:]:
        copy.wait()

    eye = lax.broadcasted_iota(jnp.int32, (ROWS, D_HEAD), 0) == lax.broadcasted_iota(
        jnp.int32, (ROWS, D_HEAD), 1
    )

    def as_row(column):
        return jnp.sum(jnp.where(eye, column, 0.0), axis=0, keepdims=True)

    def as_column(row):
        return jnp.sum(jnp.where(eye, row, 0.0), axis=1, keepdims=True)

    def in_three(row):
        first = row.astype(BF16).astype(F32)
        second = (row - first).astype(BF16).astype(F32)
        return [first, second, row - first - second]

    def message(summed, peak, total):
        rows = [summed, *in_three(as_row(peak)), *in_three(as_row(total))]
        rows.append(jnp.zeros((PART - ROWS - 6, D_HEAD), F32))
        return jnp.concatenate(rows, axis=0).astype(BF16)

    def left_over(summed):
        return (summed - summed.astype(BF16).astype(F32)).astype(BF16)

    def at_home(r):
        wait_here(home_kv.at[:, r], home_sem.at[r])
        q = q_own[r]
        scores = scores_of(spread(q), home_kv[0, r], lengths[pool * RANKS + r])
        peak = jnp.max(scores, axis=1, keepdims=True)
        q = q.astype(F32)
        new_k, new_v = nk[r].astype(F32), nv[r].astype(F32)
        steps = lax.broadcasted_iota(jnp.int32, (ROWS, 1), 0) // HEADS

        def of_new(x, j):
            shape = (ROWS, D_HEAD)
            left = jnp.broadcast_to(x[j : j + 1, :D_HEAD], shape)
            return by_head(left, jnp.broadcast_to(x[j : j + 1, D_HEAD:], shape))

        fresh = []
        for j in range(STEPS):
            score = jnp.sum(q * of_new(new_k, j), axis=1, keepdims=True)
            fresh.append(jnp.where(steps >= j, score, FLOOR))
            peak = jnp.maximum(peak, fresh[j])
        total, summed = weigh(scores, peak, home_kv[1, r])
        for j in range(STEPS):
            weight = jnp.exp2((fresh[j] - peak) * SCALE)
            total = total + weight
            summed = summed + weight.astype(BF16).astype(F32) * of_new(new_v, j)
        part[r, HOME_AT : HOME_AT + PART] = message(summed, peak, total)
        part[r, HOME_AT + PART :] = left_over(summed)
        here, there = part.at[r, pl.ds(HOME_AT, PART + ROWS)], back.at[r, pl.ds(HOME_AT, PART + ROWS)]
        remote(here, there, part_send, part_recv.at[r], joiner_of(pool), tp).start()

    for r in range(RANKS):
        at_home(r)

    wait_here(lent_kv, lent_sem)

    def lent_slot(r, b):
        request = home_of(pool, b) * RANKS + r
        slot = lax.rem(table[request * MAXB + b], SLOTS)
        return slot, lengths[request] - HOME_LEN - b * BLOCK

    def lend(r):
        scores = []
        for b in range(MAXB):
            slot, limit = lent_slot(r, b)
            scores.append(scores_of(spread(q_far[r, b]), lent_kv[0, slot], limit))
        for b in range(MAXB):
            slot, _ = lent_slot(r, b)
            peak = jnp.max(scores[b], axis=1, keepdims=True)
            total, summed = weigh(scores[b], peak, lent_kv[1, slot])
            part[r, b * PART : (b + 1) * PART] = message(summed, peak, total)
        for b in Q_ORDER:
            to = joiner_of(home_of(pool, b))
            some = pl.ds(b * PART, PART)
            remote(part.at[r, some], back.at[r, some], part_send, part_recv.at[r], to, tp).start()

    for r in range(RANKS):
        wait_come(q_far.at[r], q_recv.at[r])
        lend(r)

    w_over = remote(w_hbm, w.at[core], w_sem.at[1], w_sem.at[0], sibling, tp)
    w_over.start()
    def join(r):
        peaks, totals, sums = [], [], []
        wait_come(back.at[r], part_recv.at[r])
        for b in range(MAXB + 1):
            rows = PART if b < MAXB else PART + ROWS
            come = back[r, b * PART : b * PART + rows].astype(F32)
            stats = come[ROWS:PART]
            sums.append(come[:ROWS] if b < MAXB else come[:ROWS] + come[PART:])
            peaks.append(as_column(stats[0:1] + stats[1:2] + stats[2:3]))
            totals.append(as_column(stats[3:4] + stats[4:5] + stats[5:6]))
        peak = functools.reduce(jnp.maximum, peaks)
        factors = [jnp.exp2((one - peak) * SCALE) for one in peaks]
        total = sum(f * one for f, one in zip(factors, totals))
        summed = sum(f * one for f, one in zip(factors, sums))
        attended[r] = (summed / total).astype(BF16)

    def spread_out(ranks):
        first, count = ranks[0], len(ranks)
        mine = attended.at[pl.ds(first, count)]
        there = gathered.at[chip, pl.ds(first, count)]

        def give(to):
            to = to * 2 + 1 - core
            remote(mine, there, ag_send, ag_recv.at[first], to, tp).start()

        give(0)
        for dy, dz in FAR_FIRST:
            to = chip_off(dy, dz)
            pl.when(to != 0)(functools.partial(give, to))

    for ranks in GROUPS:
        for r in ranks:
            join(r)
        spread_out(ranks)

    wait_here(w, w_sem.at[0])

    theirs = tp * 2 + 1 - core

    def joined_at(plane):
        return lax.rem(plane + 1, TP)

    def project(g):
        ranks = GROUPS[g]
        count = len(ranks)
        come = gathered.at[:, pl.ds(ranks[0], count)]
        wait_come(come, ag_recv.at[ranks[0]])
        for k, r in enumerate(ranks):
            rows = CHIPS * ROWS
            wide[k * rows : (k + 1) * rows] = gathered[:, r].astype(F32).reshape(rows, D_HEAD)
        lhs = jnp.concatenate(
            [
                wide[pl.ds(head, count * CHIPS * STEPS, stride=HEADS), :].astype(BF16)
                for head in range(HEADS)
            ],
            axis=1,
        )
        first, size = ranks[0] * 2 * KEPT, count * 2 * KEPT
        there = landed.at[theirs, pl.ds(first, size)]
        for half in (1, 0):
            product = jnp.dot(lhs, w[half], preferred_element_type=F32)
            for plane in range(TP):
                rows = []
                for k in range(count):
                    at = k * CHIPS * STEPS + plane * KEPT
                    rows += [product[at : at + KEPT, :D_HEAD], product[at : at + KEPT, D_HEAD:]]
                sent[plane, half, first : first + size] = jnp.concatenate(rows, axis=0).astype(BF16)
            for i in (2, 1, 3):
                plane = lax.rem(tp + i, TP)
                here = sent.at[joined_at(plane), half, pl.ds(first, size)]
                remote(here, there, rs_sem.at[0], rs_sem.at[1], chip * 2 + half, plane).start()
        here = sent.at[joined_at(tp), 1 - core, pl.ds(first, size)]
        remote(here, there, rs_sem.at[0], rs_sem.at[1], sibling, tp).start()
        landed[theirs, first : first + size] = sent[joined_at(tp), core, first : first + size]

    for g in range(len(GROUPS)):
        project(g)

    all_but_own = landed.at[pl.ds(0, 2 * TP - 1)]
    wait_come(all_but_own, rs_sem.at[1])
    for half in range(2):
        both = landed[half].astype(F32)
        for i in range(1, TP):
            both = both + landed[i * 2 + half].astype(F32)
        for r in range(RANKS):
            at = r * 2 * KEPT
            mine = [both[at : at + KEPT], both[at + KEPT : at + 2 * KEPT]]
            mine = jnp.concatenate(mine, axis=1).astype(BF16)
            for each in range(PLANE):
                at = each * STEPS
                out_ref[(each * 2 + half) * RANKS + r] = mine[at : at + STEPS]

    wait_sent(q_far, q_send)
    w_over.wait_send()
    wait_sent(part, part_send)
    wait_sent(gathered, ag_send)
    wait_sent(all_but_own, rs_sem.at[0])


def per_device(*args):
    dma = pltpu.SemaphoreType.DMA
    vmem = pltpu.VMEM
    scratch = [
        vmem((RANKS, STEPS, HEADS * D_HEAD), BF16),
        vmem((RANKS, STEPS, 2 * D_HEAD), BF16),
        vmem((RANKS, STEPS, 2 * D_HEAD), BF16),
        vmem((2, RANKS, HOME_LEN, 2 * D_HEAD), BF16),
        vmem((2, SLOTS, BLOCK, 2 * D_HEAD), BF16),
        pltpu.SMEM((POOL * RANKS,), jnp.int32),
        pltpu.SMEM((POOL * RANKS * MAXB,), jnp.int32),
        vmem((2, HEADS * D_HEAD, 2 * D_HEAD), BF16),
        vmem((RANKS, ROWS, D_HEAD), BF16),
        vmem((RANKS, MAXB, ROWS, D_HEAD), BF16),
        vmem((RANKS, HOME_AT + PART + ROWS, D_HEAD), BF16),
        vmem((RANKS, HOME_AT + PART + ROWS, D_HEAD), BF16),
        vmem((RANKS, ROWS, D_HEAD), BF16),
        vmem((CHIPS, RANKS, ROWS, D_HEAD), BF16),
        vmem((RANKS * CHIPS * ROWS, D_HEAD), F32),
        vmem((TP, 2, RANKS * 2 * KEPT, D_HEAD), BF16),
        vmem((TP * 2, RANKS * 2 * KEPT, D_HEAD), BF16),
        dma((5,)),
        dma((RANKS,)),
        dma,
        dma((2,)),
        dma,
        dma((RANKS,)),
        dma,
        dma((RANKS,)),
        dma,
        dma((2,)),
        dma((2,)),
    ]
    return pl.pallas_call(
        kernel,
        out_shape=pltpu.VMEM((POOL * RANKS // TP, STEPS, 2 * D_HEAD), BF16),
        in_specs=[pl.BlockSpec(memory_space=pl.ANY)] * len(args),
        out_specs=pl.BlockSpec(memory_space=pltpu.VMEM),
        scratch_shapes=scratch,
        compiler_params=pltpu.CompilerParams(
            collective_id=0, has_side_effects=True, vmem_limit_bytes=60 * 2**20
        ),
    )(*args)


def solution(mesh):
    return jax.shard_map(
        per_device,
        mesh=mesh,
        in_specs=(
            P("pool", None, "tp"),
            P("pool", None, "tp"),
            P("pool", None, "tp"),
            P("pool", None, "tp"),
            P("pool", None, "tp"),
            P("pool", None, "tp"),
            P("pool", None, "tp"),
            P(),
            P(),
            P("tp", "pool"),
        ),
        out_specs=P("tp", None, "pool"),
        check_vma=False,
    )
```

```python
import functools
import math

import jax
import jax.numpy as jnp
from jax import lax
from jax.experimental import pallas as pl
from jax.experimental.pallas import tpu as pltpu
from jax.sharding import PartitionSpec as P

MESH = pl.DeviceIdType.MESH
F32, BF16 = jnp.float32, jnp.bfloat16

D_HEAD = 128
MAXB = 4
RANKS = 3
STEPS = 2
GROUP = 8
HEADS = 16
ROWS = STEPS * HEADS
HOME_LEN = 2048
BLOCK = 512
SLOTS = 12
POOL = 32
TP = 4
CHIPS = POOL // 2
PLANE = CHIPS // TP
KEPT = STEPS * PLANE
PART = ROWS + 16
HOME_AT = MAXB * PART
FLOOR = -1e30
Q_ORDER = (2, 3, 1, 0)
GROUPS = ((0,), (1, 2))
FAR_FIRST = sorted(
    ((dy, dz) for dy in range(TP) for dz in range(PLANE)),
    key=lambda s: -sum(min(d, 4 - d) for d in s),
)
SCALE = math.log2(math.e) * D_HEAD**-0.5


def lender_of(pool, block):
    return lax.rem(pool + 1 + 5 * block, POOL)


def home_of(pool, block):
    return lax.rem(pool + POOL - 1 - 5 * block, POOL)


def joiner_of(pool):
    return lax.rem(pool + 2 * PLANE, POOL)


def by_head(left, right):
    parts = []
    for step in range(STEPS):
        at = step * HEADS
        parts += [left[at : at + GROUP], right[at + GROUP : at + HEADS]]
    return jnp.concatenate(parts, axis=0)


def spread(q):
    q = q.astype(F32)
    none = jnp.zeros_like(q)
    return jnp.concatenate([by_head(q, none), by_head(none, q)], axis=1).astype(BF16)


def scores_of(q_wide, keys, limit):
    scores = lax.dot_general(
        q_wide, keys, (((1,), (1,)), ((), ())), preferred_element_type=F32
    )
    places = lax.broadcasted_iota(jnp.int32, scores.shape, 1)
    return jnp.where(places < limit, scores, FLOOR)


def weigh(scores, peak, values):
    weights = jnp.exp2((scores - peak) * SCALE)
    total = jnp.sum(weights, axis=1, keepdims=True)
    summed = jnp.dot(weights.astype(BF16), values, preferred_element_type=F32)
    return total, by_head(summed[:, :D_HEAD], summed[:, D_HEAD:])


def kernel(
    q_hbm,
    nk_hbm,
    nv_hbm,
    hk_hbm,
    hv_hbm,
    lk_hbm,
    lv_hbm,
    len_hbm,
    table_hbm,
    w_hbm,
    out_ref,
    q_in,
    nk,
    nv,
    home_kv,
    lent_kv,
    lengths,
    table,
    w,
    q_own,
    q_far,
    part,
    back,
    attended,
    gathered,
    wide,
    sent,
    landed,
    small_sem,
    home_sem,
    lent_sem,
    w_sem,
    q_send,
    q_recv,
    part_send,
    part_recv,
    ag_send,
    ag_recv,
    rs_sem,
):
    pool, tp = lax.axis_index("pool"), lax.axis_index("tp")
    core, chip = lax.rem(pool, 2), pool // 2
    y, z = chip // PLANE, lax.rem(chip, PLANE)
    sibling = chip * 2 + 1 - core

    def remote(src, dst, send_sem, recv_sem, pool_to, tp_to):
        return pltpu.make_async_remote_copy(
            src_ref=src,
            dst_ref=dst,
            send_sem=send_sem,
            recv_sem=recv_sem,
            device_id=(pool_to, tp_to),
            device_id_type=MESH,
        )

    def wait_sent(ref, sem):
        remote(ref, ref, sem, sem, pool, tp).wait_send()

    def wait_come(ref, sem):
        remote(ref, ref, sem, sem, pool, tp).wait_recv()

    def wait_here(ref, sem):
        pltpu.make_async_copy(ref, ref, sem).wait()

    barrier = pltpu.get_barrier_semaphore()

    def tell(pool_to, tp_to):
        pl.semaphore_signal(barrier, inc=1, device_id=(pool_to, tp_to), device_id_type=MESH)

    def chip_off(dy, dz):
        return lax.rem(y + dy, TP) * PLANE + lax.rem(z + dz, PLANE)

    for step in (-16, -6, -11, -1):
        tell(lax.rem(pool + POOL + step, POOL), tp)

    small = [
        pltpu.make_async_copy(src, dst, small_sem.at[i])
        for i, (src, dst) in enumerate(
            [(q_hbm, q_in), (len_hbm, lengths), (table_hbm, table), (nk_hbm, nk), (nv_hbm, nv)]
        )
    ]
    for copy in small:
        copy.start()

    for step in (-7, -2, 3, 8, -8, 1):
        tell(lax.rem(pool + POOL + step, POOL), tp)
    for i in (2, 1, 3):
        for half in range(2):
            tell(chip * 2 + half, lax.rem(tp + i, TP))

    def home_copies(r):
        return (
            pltpu.make_async_copy(hk_hbm.at[r], home_kv.at[0, r], home_sem.at[r]),
            pltpu.make_async_copy(hv_hbm.at[r], home_kv.at[1, r], home_sem.at[r]),
        )

    lent_copies = (
        pltpu.make_async_copy(lk_hbm, lent_kv.at[0], lent_sem),
        pltpu.make_async_copy(lv_hbm, lent_kv.at[1], lent_sem),
    )
    w_copy = pltpu.make_async_copy(w_hbm, w.at[core], w_sem.at[0])
    for copy in (*home_copies(0), *home_copies(1), *lent_copies, *home_copies(2), w_copy):
        copy.start()

    small[0].wait()
    for r in range(RANKS):
        x = q_in[r].astype(F32)
        rows = [
            x[step : step + 1, head * D_HEAD : (head + 1) * D_HEAD]
            for step in range(STEPS)
            for head in range(HEADS)
        ]
        q_own[r] = jnp.concatenate(rows, axis=0).astype(BF16)

    pl.semaphore_wait(barrier, 10 + 2 * (TP - 1))

    for r in range(RANKS):
        for b in Q_ORDER:
            to = lender_of(pool, b)
            remote(q_own.at[r], q_far.at[r, b], q_send, q_recv.at[r], to, tp).start()

    for copy in small[1:]:
        copy.wait()

    eye = lax.broadcasted_iota(jnp.int32, (ROWS, D_HEAD), 0) == lax.broadcasted_iota(
        jnp.int32, (ROWS, D_HEAD), 1
    )

    def as_row(column):
        return jnp.sum(jnp.where(eye, column, 0.0), axis=0, keepdims=True)

    def as_column(row):
        return jnp.sum(jnp.where(eye, row, 0.0), axis=1, keepdims=True)

    def in_three(row):
        first = row.astype(BF16).astype(F32)
        second = (row - first).astype(BF16).astype(F32)
        return [first, second, row - first - second]

    def message(summed, peak, total):
        rows = [summed, *in_three(as_row(peak)), *in_three(as_row(total))]
        rows.append(jnp.zeros((PART - ROWS - 6, D_HEAD), F32))
        return jnp.concatenate(rows, axis=0).astype(BF16)

    def left_over(summed):
        return (summed - summed.astype(BF16).astype(F32)).astype(BF16)

    def at_home(r):
        wait_here(home_kv.at[:, r], home_sem.at[r])
        q = q_own[r]
        scores = scores_of(spread(q), home_kv[0, r], lengths[pool * RANKS + r])
        peak = jnp.max(scores, axis=1, keepdims=True)
        q = q.astype(F32)
        new_k, new_v = nk[r].astype(F32), nv[r].astype(F32)
        steps = lax.broadcasted_iota(jnp.int32, (ROWS, 1), 0) // HEADS

        def of_new(x, j):
            shape = (ROWS, D_HEAD)
            left = jnp.broadcast_to(x[j : j + 1, :D_HEAD], shape)
            return by_head(left, jnp.broadcast_to(x[j : j + 1, D_HEAD:], shape))

        fresh = []
        for j in range(STEPS):
            score = jnp.sum(q * of_new(new_k, j), axis=1, keepdims=True)
            fresh.append(jnp.where(steps >= j, score, FLOOR))
            peak = jnp.maximum(peak, fresh[j])
        total, summed = weigh(scores, peak, home_kv[1, r])
        for j in range(STEPS):
            weight = jnp.exp2((fresh[j] - peak) * SCALE)
            total = total + weight
            summed = summed + weight.astype(BF16).astype(F32) * of_new(new_v, j)
        part[r, HOME_AT : HOME_AT + PART] = message(summed, peak, total)
        part[r, HOME_AT + PART :] = left_over(summed)
        here, there = part.at[r, pl.ds(HOME_AT, PART + ROWS)], back.at[r, pl.ds(HOME_AT, PART + ROWS)]
        remote(here, there, part_send, part_recv.at[r], joiner_of(pool), tp).start()

    for r in range(RANKS):
        at_home(r)

    wait_here(lent_kv, lent_sem)

    def lent_slot(r, b):
        request = home_of(pool, b) * RANKS + r
        slot = lax.rem(table[request * MAXB + b], SLOTS)
        return slot, lengths[request] - HOME_LEN - b * BLOCK

    def lend(r):
        scores = []
        for b in range(MAXB):
            slot, limit = lent_slot(r, b)
            scores.append(scores_of(spread(q_far[r, b]), lent_kv[0, slot], limit))
        for b in range(MAXB):
            slot, _ = lent_slot(r, b)
            peak = jnp.max(scores[b], axis=1, keepdims=True)
            total, summed = weigh(scores[b], peak, lent_kv[1, slot])
            part[r, b * PART : (b + 1) * PART] = message(summed, peak, total)
        for b in Q_ORDER:
            to = joiner_of(home_of(pool, b))
            some = pl.ds(b * PART, PART)
            remote(part.at[r, some], back.at[r, some], part_send, part_recv.at[r], to, tp).start()

    for r in range(RANKS):
        wait_come(q_far.at[r], q_recv.at[r])
        lend(r)

    w_over = remote(w_hbm, w.at[core], w_sem.at[1], w_sem.at[0], sibling, tp)
    w_over.start()
    def join(r):
        peaks, totals, sums = [], [], []
        wait_come(back.at[r], part_recv.at[r])
        for b in range(MAXB + 1):
            rows = PART if b < MAXB else PART + ROWS
            come = back[r, b * PART : b * PART + rows].astype(F32)
            stats = come[ROWS:PART]
            sums.append(come[:ROWS] if b < MAXB else come[:ROWS] + come[PART:])
            peaks.append(as_column(stats[0:1] + stats[1:2] + stats[2:3]))
            totals.append(as_column(stats[3:4] + stats[4:5] + stats[5:6]))
        peak = functools.reduce(jnp.maximum, peaks)
        factors = [jnp.exp2((one - peak) * SCALE) for one in peaks]
        total = sum(f * one for f, one in zip(factors, totals))
        summed = sum(f * one for f, one in zip(factors, sums))
        attended[r] = (summed / total).astype(BF16)

    def spread_out(ranks):
        first, count = ranks[0], len(ranks)
        mine = attended.at[pl.ds(first, count)]
        there = gathered.at[chip, pl.ds(first, count)]

        def give(to):
            to = to * 2 + 1 - core
            remote(mine, there, ag_send, ag_recv.at[first], to, tp).start()

        give(0)
        give(1)
        give(PLANE)
        for dy, dz in FAR_FIRST:
            to = chip_off(dy, dz)
            left = jnp.logical_and(to > 1, to != PLANE)
            pl.when(left)(functools.partial(give, to))

    for ranks in GROUPS:
        for r in ranks:
            join(r)
        spread_out(ranks)

    wait_here(w, w_sem.at[0])

    theirs = tp * 2 + 1 - core

    def joined_at(plane):
        return lax.rem(plane + 1, TP)

    def project(g):
        ranks = GROUPS[g]
        count = len(ranks)
        come = gathered.at[:, pl.ds(ranks[0], count)]
        wait_come(come, ag_recv.at[ranks[0]])
        for k, r in enumerate(ranks):
            rows = CHIPS * ROWS
            wide[k * rows : (k + 1) * rows] = gathered[:, r].astype(F32).reshape(rows, D_HEAD)
        lhs = jnp.concatenate(
            [
                wide[pl.ds(head, count * CHIPS * STEPS, stride=HEADS), :].astype(BF16)
                for head in range(HEADS)
            ],
            axis=1,
        )
        first, size = ranks[0] * 2 * KEPT, count * 2 * KEPT
        there = landed.at[theirs, pl.ds(first, size)]
        for half in (1, 0):
            product = jnp.dot(lhs, w[half], preferred_element_type=F32)
            for plane in range(TP):
                rows = []
                for k in range(count):
                    at = k * CHIPS * STEPS + plane * KEPT
                    rows += [product[at : at + KEPT, :D_HEAD], product[at : at + KEPT, D_HEAD:]]
                sent[plane, half, first : first + size] = jnp.concatenate(rows, axis=0).astype(BF16)
            for i in (2, 1, 3):
                plane = lax.rem(tp + i, TP)
                here = sent.at[joined_at(plane), half, pl.ds(first, size)]
                remote(here, there, rs_sem.at[0], rs_sem.at[1], chip * 2 + half, plane).start()
        here = sent.at[joined_at(tp), 1 - core, pl.ds(first, size)]
        remote(here, there, rs_sem.at[0], rs_sem.at[1], sibling, tp).start()
        landed[theirs, first : first + size] = sent[joined_at(tp), core, first : first + size]

    for g in range(len(GROUPS)):
        project(g)

    all_but_own = landed.at[pl.ds(0, 2 * TP - 1)]
    wait_come(all_but_own, rs_sem.at[1])
    for half in range(2):
        both = landed[half].astype(F32)
        for i in range(1, TP):
            both = both + landed[i * 2 + half].astype(F32)
        for r in range(RANKS):
            at = r * 2 * KEPT
            mine = [both[at : at + KEPT], both[at + KEPT : at + 2 * KEPT]]
            mine = jnp.concatenate(mine, axis=1).astype(BF16)
            for each in range(PLANE):
                at = each * STEPS
                out_ref[(each * 2 + half) * RANKS + r] = mine[at : at + STEPS]

    wait_sent(q_far, q_send)
    w_over.wait_send()
    wait_sent(part, part_send)
    wait_sent(gathered, ag_send)
    wait_sent(all_but_own, rs_sem.at[0])


def per_device(*args):
    dma = pltpu.SemaphoreType.DMA
    vmem = pltpu.VMEM
    scratch = [
        vmem((RANKS, STEPS, HEADS * D_HEAD), BF16),
        vmem((RANKS, STEPS, 2 * D_HEAD), BF16),
        vmem((RANKS, STEPS, 2 * D_HEAD), BF16),
        vmem((2, RANKS, HOME_LEN, 2 * D_HEAD), BF16),
        vmem((2, SLOTS, BLOCK, 2 * D_HEAD), BF16),
        pltpu.SMEM((POOL * RANKS,), jnp.int32),
        pltpu.SMEM((POOL * RANKS * MAXB,), jnp.int32),
        vmem((2, HEADS * D_HEAD, 2 * D_HEAD), BF16),
        vmem((RANKS, ROWS, D_HEAD), BF16),
        vmem((RANKS, MAXB, ROWS, D_HEAD), BF16),
        vmem((RANKS, HOME_AT + PART + ROWS, D_HEAD), BF16),
        vmem((RANKS, HOME_AT + PART + ROWS, D_HEAD), BF16),
        vmem((RANKS, ROWS, D_HEAD), BF16),
        vmem((CHIPS, RANKS, ROWS, D_HEAD), BF16),
        vmem((RANKS * CHIPS * ROWS, D_HEAD), F32),
        vmem((TP, 2, RANKS * 2 * KEPT, D_HEAD), BF16),
        vmem((TP * 2, RANKS * 2 * KEPT, D_HEAD), BF16),
        dma((5,)),
        dma((RANKS,)),
        dma,
        dma((2,)),
        dma,
        dma((RANKS,)),
        dma,
        dma((RANKS,)),
        dma,
        dma((2,)),
        dma((2,)),
    ]
    return pl.pallas_call(
        kernel,
        out_shape=pltpu.VMEM((POOL * RANKS // TP, STEPS, 2 * D_HEAD), BF16),
        in_specs=[pl.BlockSpec(memory_space=pl.ANY)] * len(args),
        out_specs=pl.BlockSpec(memory_space=pltpu.VMEM),
        scratch_shapes=scratch,
        compiler_params=pltpu.CompilerParams(
            collective_id=0, has_side_effects=True, vmem_limit_bytes=60 * 2**20
        ),
    )(*args)


def solution(mesh):
    return jax.shard_map(
        per_device,
        mesh=mesh,
        in_specs=(
            P("pool", None, "tp"),
            P("pool", None, "tp"),
            P("pool", None, "tp"),
            P("pool", None, "tp"),
            P("pool", None, "tp"),
            P("pool", None, "tp"),
            P("pool", None, "tp"),
            P(),
            P(),
            P("tp", "pool"),
        ),
        out_specs=P("tp", None, "pool"),
        check_vma=False,
    )
```

```python
import functools
import math

import jax
import jax.numpy as jnp
from jax import lax
from jax.experimental import pallas as pl
from jax.experimental.pallas import tpu as pltpu
from jax.sharding import PartitionSpec as P

MESH = pl.DeviceIdType.MESH
F32, BF16 = jnp.float32, jnp.bfloat16

D_HEAD = 128
MAXB = 4
RANKS = 3
STEPS = 2
GROUP = 8
HEADS = 16
ROWS = STEPS * HEADS
HOME_LEN = 2048
BLOCK = 512
SLOTS = 12
POOL = 32
TP = 4
CHIPS = POOL // 2
PLANE = CHIPS // TP
KEPT = STEPS * PLANE
PART = ROWS + 16
HOME_AT = MAXB * PART
FLOOR = -1e30
Q_ORDER = (2, 1, 3, 0)
GROUPS = ((0,), (1, 2))
FAR_FIRST = sorted(
    ((dy, dz) for dy in range(TP) for dz in range(PLANE)),
    key=lambda s: -sum(min(d, 4 - d) for d in s),
)
SCALE = math.log2(math.e) * D_HEAD**-0.5


def lender_of(pool, block):
    return lax.rem(pool + 1 + 5 * block, POOL)


def home_of(pool, block):
    return lax.rem(pool + POOL - 1 - 5 * block, POOL)


def joiner_of(pool):
    return lax.rem(pool + 2 * PLANE, POOL)


def by_head(left, right):
    parts = []
    for step in range(STEPS):
        at = step * HEADS
        parts += [left[at : at + GROUP], right[at + GROUP : at + HEADS]]
    return jnp.concatenate(parts, axis=0)


def spread(q):
    q = q.astype(F32)
    none = jnp.zeros_like(q)
    return jnp.concatenate([by_head(q, none), by_head(none, q)], axis=1).astype(BF16)


def scores_of(q_wide, keys, limit):
    scores = lax.dot_general(
        q_wide, keys, (((1,), (1,)), ((), ())), preferred_element_type=F32
    )
    places = lax.broadcasted_iota(jnp.int32, scores.shape, 1)
    return jnp.where(places < limit, scores, FLOOR)


def weigh(scores, peak, values):
    weights = jnp.exp2((scores - peak) * SCALE)
    total = jnp.sum(weights, axis=1, keepdims=True)
    summed = jnp.dot(weights.astype(BF16), values, preferred_element_type=F32)
    return total, by_head(summed[:, :D_HEAD], summed[:, D_HEAD:])


def kernel(
    q_hbm,
    nk_hbm,
    nv_hbm,
    hk_hbm,
    hv_hbm,
    lk_hbm,
    lv_hbm,
    len_hbm,
    table_hbm,
    w_hbm,
    out_ref,
    q_in,
    nk,
    nv,
    home_kv,
    lent_kv,
    lengths,
    table,
    w,
    q_own,
    q_far,
    part,
    back,
    attended,
    gathered,
    wide,
    sent,
    landed,
    small_sem,
    home_sem,
    lent_sem,
    w_sem,
    q_send,
    q_recv,
    part_send,
    part_recv,
    ag_send,
    ag_recv,
    rs_sem,
):
    pool, tp = lax.axis_index("pool"), lax.axis_index("tp")
    core, chip = lax.rem(pool, 2), pool // 2
    y, z = chip // PLANE, lax.rem(chip, PLANE)
    sibling = chip * 2 + 1 - core

    def remote(src, dst, send_sem, recv_sem, pool_to, tp_to):
        return pltpu.make_async_remote_copy(
            src_ref=src,
            dst_ref=dst,
            send_sem=send_sem,
            recv_sem=recv_sem,
            device_id=(pool_to, tp_to),
            device_id_type=MESH,
        )

    def wait_sent(ref, sem):
        remote(ref, ref, sem, sem, pool, tp).wait_send()

    def wait_come(ref, sem):
        remote(ref, ref, sem, sem, pool, tp).wait_recv()

    def wait_here(ref, sem):
        pltpu.make_async_copy(ref, ref, sem).wait()

    barrier = pltpu.get_barrier_semaphore()

    def tell(pool_to, tp_to):
        pl.semaphore_signal(barrier, inc=1, device_id=(pool_to, tp_to), device_id_type=MESH)

    def chip_off(dy, dz):
        return lax.rem(y + dy, TP) * PLANE + lax.rem(z + dz, PLANE)

    for step in (-16, -6, -11, -1):
        tell(lax.rem(pool + POOL + step, POOL), tp)

    small = [
        pltpu.make_async_copy(src, dst, small_sem.at[i])
        for i, (src, dst) in enumerate(
            [(q_hbm, q_in), (len_hbm, lengths), (table_hbm, table), (nk_hbm, nk), (nv_hbm, nv)]
        )
    ]
    for copy in small:
        copy.start()

    for step in (-7, -2, 3, 8, -8, 1):
        tell(lax.rem(pool + POOL + step, POOL), tp)
    for i in (2, 1, 3):
        for half in range(2):
            tell(chip * 2 + half, lax.rem(tp + i, TP))

    def home_copies(r):
        return (
            pltpu.make_async_copy(hk_hbm.at[r], home_kv.at[0, r], home_sem.at[r]),
            pltpu.make_async_copy(hv_hbm.at[r], home_kv.at[1, r], home_sem.at[r]),
        )

    lent_copies = (
        pltpu.make_async_copy(lk_hbm, lent_kv.at[0], lent_sem),
        pltpu.make_async_copy(lv_hbm, lent_kv.at[1], lent_sem),
    )
    w_copy = pltpu.make_async_copy(w_hbm, w.at[core], w_sem.at[0])
    for copy in (*home_copies(0), *home_copies(1), *lent_copies, *home_copies(2), w_copy):
        copy.start()

    small[0].wait()
    for r in range(RANKS):
        x = q_in[r].astype(F32)
        rows = [
            x[step : step + 1, head * D_HEAD : (head + 1) * D_HEAD]
            for step in range(STEPS)
            for head in range(HEADS)
        ]
        q_own[r] = jnp.concatenate(rows, axis=0).astype(BF16)

    pl.semaphore_wait(barrier, 10 + 2 * (TP - 1))

    for r in range(RANKS):
        for b in Q_ORDER:
            to = lender_of(pool, b)
            remote(q_own.at[r], q_far.at[r, b], q_send, q_recv.at[r], to, tp).start()

    for copy in small[1:]:
        copy.wait()

    eye = lax.broadcasted_iota(jnp.int32, (ROWS, D_HEAD), 0) == lax.broadcasted_iota(
        jnp.int32, (ROWS, D_HEAD), 1
    )

    def as_row(column):
        return jnp.sum(jnp.where(eye, column, 0.0), axis=0, keepdims=True)

    def as_column(row):
        return jnp.sum(jnp.where(eye, row, 0.0), axis=1, keepdims=True)

    def in_three(row):
        first = row.astype(BF16).astype(F32)
        second = (row - first).astype(BF16).astype(F32)
        return [first, second, row - first - second]

    def message(summed, peak, total):
        rows = [summed, *in_three(as_row(peak)), *in_three(as_row(total))]
        rows.append(jnp.zeros((PART - ROWS - 6, D_HEAD), F32))
        return jnp.concatenate(rows, axis=0).astype(BF16)

    def left_over(summed):
        return (summed - summed.astype(BF16).astype(F32)).astype(BF16)

    def at_home(r):
        wait_here(home_kv.at[:, r], home_sem.at[r])
        q = q_own[r]
        scores = scores_of(spread(q), home_kv[0, r], lengths[pool * RANKS + r])
        peak = jnp.max(scores, axis=1, keepdims=True)
        q = q.astype(F32)
        new_k, new_v = nk[r].astype(F32), nv[r].astype(F32)
        steps = lax.broadcasted_iota(jnp.int32, (ROWS, 1), 0) // HEADS

        def of_new(x, j):
            shape = (ROWS, D_HEAD)
            left = jnp.broadcast_to(x[j : j + 1, :D_HEAD], shape)
            return by_head(left, jnp.broadcast_to(x[j : j + 1, D_HEAD:], shape))

        fresh = []
        for j in range(STEPS):
            score = jnp.sum(q * of_new(new_k, j), axis=1, keepdims=True)
            fresh.append(jnp.where(steps >= j, score, FLOOR))
            peak = jnp.maximum(peak, fresh[j])
        total, summed = weigh(scores, peak, home_kv[1, r])
        for j in range(STEPS):
            weight = jnp.exp2((fresh[j] - peak) * SCALE)
            total = total + weight
            summed = summed + weight.astype(BF16).astype(F32) * of_new(new_v, j)
        part[r, HOME_AT : HOME_AT + PART] = message(summed, peak, total)
        part[r, HOME_AT + PART :] = left_over(summed)
        here, there = part.at[r, pl.ds(HOME_AT, PART + ROWS)], back.at[r, pl.ds(HOME_AT, PART + ROWS)]
        remote(here, there, part_send, part_recv.at[r], joiner_of(pool), tp).start()

    for r in range(RANKS):
        at_home(r)

    wait_here(lent_kv, lent_sem)

    def lent_slot(r, b):
        request = home_of(pool, b) * RANKS + r
        slot = lax.rem(table[request * MAXB + b], SLOTS)
        return slot, lengths[request] - HOME_LEN - b * BLOCK

    def lend(r):
        scores = []
        for b in range(MAXB):
            slot, limit = lent_slot(r, b)
            scores.append(scores_of(spread(q_far[r, b]), lent_kv[0, slot], limit))
        for b in range(MAXB):
            slot, _ = lent_slot(r, b)
            peak = jnp.max(scores[b], axis=1, keepdims=True)
            total, summed = weigh(scores[b], peak, lent_kv[1, slot])
            part[r, b * PART : (b + 1) * PART] = message(summed, peak, total)
        for b in Q_ORDER:
            to = joiner_of(home_of(pool, b))
            some = pl.ds(b * PART, PART)
            remote(part.at[r, some], back.at[r, some], part_send, part_recv.at[r], to, tp).start()

    for r in range(RANKS):
        wait_come(q_far.at[r], q_recv.at[r])
        lend(r)

    w_over = remote(w_hbm, w.at[core], w_sem.at[1], w_sem.at[0], sibling, tp)
    w_over.start()
    def join(r):
        peaks, totals, sums = [], [], []
        wait_come(back.at[r], part_recv.at[r])
        for b in range(MAXB + 1):
            rows = PART if b < MAXB else PART + ROWS
            come = back[r, b * PART : b * PART + rows].astype(F32)
            stats = come[ROWS:PART]
            sums.append(come[:ROWS] if b < MAXB else come[:ROWS] + come[PART:])
            peaks.append(as_column(stats[0:1] + stats[1:2] + stats[2:3]))
            totals.append(as_column(stats[3:4] + stats[4:5] + stats[5:6]))
        peak = functools.reduce(jnp.maximum, peaks)
        factors = [jnp.exp2((one - peak) * SCALE) for one in peaks]
        total = sum(f * one for f, one in zip(factors, totals))
        summed = sum(f * one for f, one in zip(factors, sums))
        attended[r] = (summed / total).astype(BF16)

    def spread_out(ranks):
        first, count = ranks[0], len(ranks)
        mine = attended.at[pl.ds(first, count)]
        there = gathered.at[chip, pl.ds(first, count)]

        def give(to):
            to = to * 2 + 1 - core
            remote(mine, there, ag_send, ag_recv.at[first], to, tp).start()

        give(0)
        give(1)
        give(PLANE)
        for dy, dz in FAR_FIRST:
            to = chip_off(dy, dz)
            left = jnp.logical_and(to > 1, to != PLANE)
            pl.when(left)(functools.partial(give, to))

    for ranks in GROUPS:
        for r in ranks:
            join(r)
        spread_out(ranks)

    wait_here(w, w_sem.at[0])

    theirs = tp * 2 + 1 - core

    def joined_at(plane):
        return lax.rem(plane + 1, TP)

    def project(g):
        ranks = GROUPS[g]
        count = len(ranks)
        come = gathered.at[:, pl.ds(ranks[0], count)]
        wait_come(come, ag_recv.at[ranks[0]])
        for k, r in enumerate(ranks):
            rows = CHIPS * ROWS
            wide[k * rows : (k + 1) * rows] = gathered[:, r].astype(F32).reshape(rows, D_HEAD)
        lhs = jnp.concatenate(
            [
                wide[pl.ds(head, count * CHIPS * STEPS, stride=HEADS), :].astype(BF16)
                for head in range(HEADS)
            ],
            axis=1,
        )
        first, size = ranks[0] * 2 * KEPT, count * 2 * KEPT
        there = landed.at[theirs, pl.ds(first, size)]
        for half in (1, 0):
            product = jnp.dot(lhs, w[half], preferred_element_type=F32)
            for plane in range(TP):
                rows = []
                for k in range(count):
                    at = k * CHIPS * STEPS + plane * KEPT
                    rows += [product[at : at + KEPT, :D_HEAD], product[at : at + KEPT, D_HEAD:]]
                sent[plane, half, first : first + size] = jnp.concatenate(rows, axis=0).astype(BF16)
            for i in (2, 1, 3):
                plane = lax.rem(tp + i, TP)
                here = sent.at[joined_at(plane), half, pl.ds(first, size)]
                remote(here, there, rs_sem.at[0], rs_sem.at[1], chip * 2 + half, plane).start()
        here = sent.at[joined_at(tp), 1 - core, pl.ds(first, size)]
        remote(here, there, rs_sem.at[0], rs_sem.at[1], sibling, tp).start()
        landed[theirs, first : first + size] = sent[joined_at(tp), core, first : first + size]

    for g in range(len(GROUPS)):
        project(g)

    all_but_own = landed.at[pl.ds(0, 2 * TP - 1)]
    wait_come(all_but_own, rs_sem.at[1])
    for half in range(2):
        both = landed[half].astype(F32)
        for i in range(1, TP):
            both = both + landed[i * 2 + half].astype(F32)
        for r in range(RANKS):
            at = r * 2 * KEPT
            mine = [both[at : at + KEPT], both[at + KEPT : at + 2 * KEPT]]
            mine = jnp.concatenate(mine, axis=1).astype(BF16)
            for each in range(PLANE):
                at = each * STEPS
                out_ref[(each * 2 + half) * RANKS + r] = mine[at : at + STEPS]

    wait_sent(q_far, q_send)
    w_over.wait_send()
    wait_sent(part, part_send)
    wait_sent(gathered, ag_send)
    wait_sent(all_but_own, rs_sem.at[0])


def per_device(*args):
    dma = pltpu.SemaphoreType.DMA
    vmem = pltpu.VMEM
    scratch = [
        vmem((RANKS, STEPS, HEADS * D_HEAD), BF16),
        vmem((RANKS, STEPS, 2 * D_HEAD), BF16),
        vmem((RANKS, STEPS, 2 * D_HEAD), BF16),
        vmem((2, RANKS, HOME_LEN, 2 * D_HEAD), BF16),
        vmem((2, SLOTS, BLOCK, 2 * D_HEAD), BF16),
        pltpu.SMEM((POOL * RANKS,), jnp.int32),
        pltpu.SMEM((POOL * RANKS * MAXB,), jnp.int32),
        vmem((2, HEADS * D_HEAD, 2 * D_HEAD), BF16),
        vmem((RANKS, ROWS, D_HEAD), BF16),
        vmem((RANKS, MAXB, ROWS, D_HEAD), BF16),
        vmem((RANKS, HOME_AT + PART + ROWS, D_HEAD), BF16),
        vmem((RANKS, HOME_AT + PART + ROWS, D_HEAD), BF16),
        vmem((RANKS, ROWS, D_HEAD), BF16),
        vmem((CHIPS, RANKS, ROWS, D_HEAD), BF16),
        vmem((RANKS * CHIPS * ROWS, D_HEAD), F32),
        vmem((TP, 2, RANKS * 2 * KEPT, D_HEAD), BF16),
        vmem((TP * 2, RANKS * 2 * KEPT, D_HEAD), BF16),
        dma((5,)),
        dma((RANKS,)),
        dma,
        dma((2,)),
        dma,
        dma((RANKS,)),
        dma,
        dma((RANKS,)),
        dma,
        dma((2,)),
        dma((2,)),
    ]
    return pl.pallas_call(
        kernel,
        out_shape=pltpu.VMEM((POOL * RANKS // TP, STEPS, 2 * D_HEAD), BF16),
        in_specs=[pl.BlockSpec(memory_space=pl.ANY)] * len(args),
        out_specs=pl.BlockSpec(memory_space=pltpu.VMEM),
        scratch_shapes=scratch,
        compiler_params=pltpu.CompilerParams(
            collective_id=0, has_side_effects=True, vmem_limit_bytes=60 * 2**20
        ),
    )(*args)


def solution(mesh):
    return jax.shard_map(
        per_device,
        mesh=mesh,
        in_specs=(
            P("pool", None, "tp"),
            P("pool", None, "tp"),
            P("pool", None, "tp"),
            P("pool", None, "tp"),
            P("pool", None, "tp"),
            P("pool", None, "tp"),
            P("pool", None, "tp"),
            P(),
            P(),
            P("tp", "pool"),
        ),
        out_specs=P("tp", None, "pool"),
        check_vma=False,
    )
```

```python
import functools
import math

import jax
import jax.numpy as jnp
from jax import lax
from jax.experimental import pallas as pl
from jax.experimental.pallas import tpu as pltpu
from jax.sharding import PartitionSpec as P

MESH = pl.DeviceIdType.MESH
F32, BF16 = jnp.float32, jnp.bfloat16

D_HEAD = 128
MAXB = 4
RANKS = 3
STEPS = 2
GROUP = 8
HEADS = 16
ROWS = STEPS * HEADS
HOME_LEN = 2048
BLOCK = 512
SLOTS = 12
POOL = 32
TP = 4
CHIPS = POOL // 2
PLANE = CHIPS // TP
KEPT = STEPS * PLANE
PART = ROWS + 16
HOME_AT = MAXB * PART
FLOOR = -1e30
Q_ORDER = (1, 2, 3, 0)
GROUPS = ((0,), (1, 2))
FAR_FIRST = sorted(
    ((dy, dz) for dy in range(TP) for dz in range(PLANE)),
    key=lambda s: -sum(min(d, 4 - d) for d in s),
)
SCALE = math.log2(math.e) * D_HEAD**-0.5


def lender_of(pool, block):
    return lax.rem(pool + 1 + 5 * block, POOL)


def home_of(pool, block):
    return lax.rem(pool + POOL - 1 - 5 * block, POOL)


def joiner_of(pool):
    return lax.rem(pool + 2 * PLANE, POOL)


def by_head(left, right):
    parts = []
    for step in range(STEPS):
        at = step * HEADS
        parts += [left[at : at + GROUP], right[at + GROUP : at + HEADS]]
    return jnp.concatenate(parts, axis=0)


def spread(q):
    q = q.astype(F32)
    none = jnp.zeros_like(q)
    return jnp.concatenate([by_head(q, none), by_head(none, q)], axis=1).astype(BF16)


def scores_of(q_wide, keys, limit):
    scores = lax.dot_general(
        q_wide, keys, (((1,), (1,)), ((), ())), preferred_element_type=F32
    )
    places = lax.broadcasted_iota(jnp.int32, scores.shape, 1)
    return jnp.where(places < limit, scores, FLOOR)


def weigh(scores, peak, values):
    weights = jnp.exp2((scores - peak) * SCALE)
    total = jnp.sum(weights, axis=1, keepdims=True)
    summed = jnp.dot(weights.astype(BF16), values, preferred_element_type=F32)
    return total, by_head(summed[:, :D_HEAD], summed[:, D_HEAD:])


def kernel(
    q_hbm,
    nk_hbm,
    nv_hbm,
    hk_hbm,
    hv_hbm,
    lk_hbm,
    lv_hbm,
    len_hbm,
    table_hbm,
    w_hbm,
    out_ref,
    q_in,
    nk,
    nv,
    home_kv,
    lent_kv,
    lengths,
    table,
    w,
    q_own,
    q_far,
    part,
    back,
    attended,
    gathered,
    wide,
    sent,
    landed,
    small_sem,
    home_sem,
    lent_sem,
    w_sem,
    q_send,
    q_recv,
    part_send,
    part_recv,
    ag_send,
    ag_recv,
    rs_sem,
):
    pool, tp = lax.axis_index("pool"), lax.axis_index("tp")
    core, chip = lax.rem(pool, 2), pool // 2
    y, z = chip // PLANE, lax.rem(chip, PLANE)
    sibling = chip * 2 + 1 - core

    def remote(src, dst, send_sem, recv_sem, pool_to, tp_to):
        return pltpu.make_async_remote_copy(
            src_ref=src,
            dst_ref=dst,
            send_sem=send_sem,
            recv_sem=recv_sem,
            device_id=(pool_to, tp_to),
            device_id_type=MESH,
        )

    def wait_sent(ref, sem):
        remote(ref, ref, sem, sem, pool, tp).wait_send()

    def wait_come(ref, sem):
        remote(ref, ref, sem, sem, pool, tp).wait_recv()

    def wait_here(ref, sem):
        pltpu.make_async_copy(ref, ref, sem).wait()

    barrier = pltpu.get_barrier_semaphore()

    def tell(pool_to, tp_to):
        pl.semaphore_signal(barrier, inc=1, device_id=(pool_to, tp_to), device_id_type=MESH)

    def chip_off(dy, dz):
        return lax.rem(y + dy, TP) * PLANE + lax.rem(z + dz, PLANE)

    for step in (-16, -6, -11, -1):
        tell(lax.rem(pool + POOL + step, POOL), tp)

    small = [
        pltpu.make_async_copy(src, dst, small_sem.at[i])
        for i, (src, dst) in enumerate(
            [(q_hbm, q_in), (len_hbm, lengths), (table_hbm, table), (nk_hbm, nk), (nv_hbm, nv)]
        )
    ]
    for copy in small:
        copy.start()

    for step in (-7, -2, 3, 8, -8, 1):
        tell(lax.rem(pool + POOL + step, POOL), tp)
    for i in (2, 1, 3):
        for half in range(2):
            tell(chip * 2 + half, lax.rem(tp + i, TP))

    def home_copies(r):
        return (
            pltpu.make_async_copy(hk_hbm.at[r], home_kv.at[0, r], home_sem.at[r]),
            pltpu.make_async_copy(hv_hbm.at[r], home_kv.at[1, r], home_sem.at[r]),
        )

    lent_copies = (
        pltpu.make_async_copy(lk_hbm, lent_kv.at[0], lent_sem),
        pltpu.make_async_copy(lv_hbm, lent_kv.at[1], lent_sem),
    )
    w_copy = pltpu.make_async_copy(w_hbm, w.at[core], w_sem.at[0])
    for copy in (*home_copies(0), *home_copies(1), *lent_copies, *home_copies(2), w_copy):
        copy.start()

    small[0].wait()
    for r in range(RANKS):
        x = q_in[r].astype(F32)
        rows = [
            x[step : step + 1, head * D_HEAD : (head + 1) * D_HEAD]
            for step in range(STEPS)
            for head in range(HEADS)
        ]
        q_own[r] = jnp.concatenate(rows, axis=0).astype(BF16)

    pl.semaphore_wait(barrier, 10 + 2 * (TP - 1))

    for r in range(RANKS):
        for b in Q_ORDER:
            to = lender_of(pool, b)
            remote(q_own.at[r], q_far.at[r, b], q_send, q_recv.at[r], to, tp).start()

    for copy in small[1:]:
        copy.wait()

    eye = lax.broadcasted_iota(jnp.int32, (ROWS, D_HEAD), 0) == lax.broadcasted_iota(
        jnp.int32, (ROWS, D_HEAD), 1
    )

    def as_row(column):
        return jnp.sum(jnp.where(eye, column, 0.0), axis=0, keepdims=True)

    def as_column(row):
        return jnp.sum(jnp.where(eye, row, 0.0), axis=1, keepdims=True)

    def in_three(row):
        first = row.astype(BF16).astype(F32)
        second = (row - first).astype(BF16).astype(F32)
        return [first, second, row - first - second]

    def message(summed, peak, total):
        rows = [summed, *in_three(as_row(peak)), *in_three(as_row(total))]
        rows.append(jnp.zeros((PART - ROWS - 6, D_HEAD), F32))
        return jnp.concatenate(rows, axis=0).astype(BF16)

    def left_over(summed):
        return (summed - summed.astype(BF16).astype(F32)).astype(BF16)

    def at_home(r):
        wait_here(home_kv.at[:, r], home_sem.at[r])
        q = q_own[r]
        scores = scores_of(spread(q), home_kv[0, r], lengths[pool * RANKS + r])
        peak = jnp.max(scores, axis=1, keepdims=True)
        q = q.astype(F32)
        new_k, new_v = nk[r].astype(F32), nv[r].astype(F32)
        steps = lax.broadcasted_iota(jnp.int32, (ROWS, 1), 0) // HEADS

        def of_new(x, j):
            shape = (ROWS, D_HEAD)
            left = jnp.broadcast_to(x[j : j + 1, :D_HEAD], shape)
            return by_head(left, jnp.broadcast_to(x[j : j + 1, D_HEAD:], shape))

        fresh = []
        for j in range(STEPS):
            score = jnp.sum(q * of_new(new_k, j), axis=1, keepdims=True)
            fresh.append(jnp.where(steps >= j, score, FLOOR))
            peak = jnp.maximum(peak, fresh[j])
        total, summed = weigh(scores, peak, home_kv[1, r])
        for j in range(STEPS):
            weight = jnp.exp2((fresh[j] - peak) * SCALE)
            total = total + weight
            summed = summed + weight.astype(BF16).astype(F32) * of_new(new_v, j)
        part[r, HOME_AT : HOME_AT + PART] = message(summed, peak, total)
        part[r, HOME_AT + PART :] = left_over(summed)
        here, there = part.at[r, pl.ds(HOME_AT, PART + ROWS)], back.at[r, pl.ds(HOME_AT, PART + ROWS)]
        remote(here, there, part_send, part_recv.at[r], joiner_of(pool), tp).start()

    for r in range(RANKS):
        at_home(r)

    wait_here(lent_kv, lent_sem)

    def lent_slot(r, b):
        request = home_of(pool, b) * RANKS + r
        slot = lax.rem(table[request * MAXB + b], SLOTS)
        return slot, lengths[request] - HOME_LEN - b * BLOCK

    def lend(r):
        scores = []
        for b in range(MAXB):
            slot, limit = lent_slot(r, b)
            scores.append(scores_of(spread(q_far[r, b]), lent_kv[0, slot], limit))
        for b in range(MAXB):
            slot, _ = lent_slot(r, b)
            peak = jnp.max(scores[b], axis=1, keepdims=True)
            total, summed = weigh(scores[b], peak, lent_kv[1, slot])
            part[r, b * PART : (b + 1) * PART] = message(summed, peak, total)
        for b in Q_ORDER:
            to = joiner_of(home_of(pool, b))
            some = pl.ds(b * PART, PART)
            remote(part.at[r, some], back.at[r, some], part_send, part_recv.at[r], to, tp).start()

    for r in range(RANKS):
        wait_come(q_far.at[r], q_recv.at[r])
        lend(r)

    w_over = remote(w_hbm, w.at[core], w_sem.at[1], w_sem.at[0], sibling, tp)
    w_over.start()
    def join(r):
        peaks, totals, sums = [], [], []
        wait_come(back.at[r], part_recv.at[r])
        for b in range(MAXB + 1):
            rows = PART if b < MAXB else PART + ROWS
            come = back[r, b * PART : b * PART + rows].astype(F32)
            stats = come[ROWS:PART]
            sums.append(come[:ROWS] if b < MAXB else come[:ROWS] + come[PART:])
            peaks.append(as_column(stats[0:1] + stats[1:2] + stats[2:3]))
            totals.append(as_column(stats[3:4] + stats[4:5] + stats[5:6]))
        peak = functools.reduce(jnp.maximum, peaks)
        factors = [jnp.exp2((one - peak) * SCALE) for one in peaks]
        total = sum(f * one for f, one in zip(factors, totals))
        summed = sum(f * one for f, one in zip(factors, sums))
        attended[r] = (summed / total).astype(BF16)

    def spread_out(ranks):
        first, count = ranks[0], len(ranks)
        mine = attended.at[pl.ds(first, count)]
        there = gathered.at[chip, pl.ds(first, count)]

        def give(to):
            to = to * 2 + 1 - core
            remote(mine, there, ag_send, ag_recv.at[first], to, tp).start()

        give(0)
        give(1)
        give(PLANE)
        for dy, dz in FAR_FIRST:
            to = chip_off(dy, dz)
            left = jnp.logical_and(to > 1, to != PLANE)
            pl.when(left)(functools.partial(give, to))

    for ranks in GROUPS:
        for r in ranks:
            join(r)
        spread_out(ranks)

    wait_here(w, w_sem.at[0])

    theirs = tp * 2 + 1 - core

    def joined_at(plane):
        return lax.rem(plane + 1, TP)

    def project(g):
        ranks = GROUPS[g]
        count = len(ranks)
        come = gathered.at[:, pl.ds(ranks[0], count)]
        wait_come(come, ag_recv.at[ranks[0]])
        for k, r in enumerate(ranks):
            rows = CHIPS * ROWS
            wide[k * rows : (k + 1) * rows] = gathered[:, r].astype(F32).reshape(rows, D_HEAD)
        lhs = jnp.concatenate(
            [
                wide[pl.ds(head, count * CHIPS * STEPS, stride=HEADS), :].astype(BF16)
                for head in range(HEADS)
            ],
            axis=1,
        )
        first, size = ranks[0] * 2 * KEPT, count * 2 * KEPT
        there = landed.at[theirs, pl.ds(first, size)]
        for half in (1, 0):
            product = jnp.dot(lhs, w[half], preferred_element_type=F32)
            for plane in range(TP):
                rows = []
                for k in range(count):
                    at = k * CHIPS * STEPS + plane * KEPT
                    rows += [product[at : at + KEPT, :D_HEAD], product[at : at + KEPT, D_HEAD:]]
                sent[plane, half, first : first + size] = jnp.concatenate(rows, axis=0).astype(BF16)
            for i in (2, 1, 3):
                plane = lax.rem(tp + i, TP)
                here = sent.at[joined_at(plane), half, pl.ds(first, size)]
                remote(here, there, rs_sem.at[0], rs_sem.at[1], chip * 2 + half, plane).start()
        here = sent.at[joined_at(tp), 1 - core, pl.ds(first, size)]
        remote(here, there, rs_sem.at[0], rs_sem.at[1], sibling, tp).start()
        landed[theirs, first : first + size] = sent[joined_at(tp), core, first : first + size]

    for g in range(len(GROUPS)):
        project(g)

    all_but_own = landed.at[pl.ds(0, 2 * TP - 1)]
    wait_come(all_but_own, rs_sem.at[1])
    for half in range(2):
        both = landed[half].astype(F32)
        for i in range(1, TP):
            both = both + landed[i * 2 + half].astype(F32)
        for r in range(RANKS):
            at = r * 2 * KEPT
            mine = [both[at : at + KEPT], both[at + KEPT : at + 2 * KEPT]]
            mine = jnp.concatenate(mine, axis=1).astype(BF16)
            for each in range(PLANE):
                at = each * STEPS
                out_ref[(each * 2 + half) * RANKS + r] = mine[at : at + STEPS]

    wait_sent(q_far, q_send)
    w_over.wait_send()
    wait_sent(part, part_send)
    wait_sent(gathered, ag_send)
    wait_sent(all_but_own, rs_sem.at[0])


def per_device(*args):
    dma = pltpu.SemaphoreType.DMA
    vmem = pltpu.VMEM
    scratch = [
        vmem((RANKS, STEPS, HEADS * D_HEAD), BF16),
        vmem((RANKS, STEPS, 2 * D_HEAD), BF16),
        vmem((RANKS, STEPS, 2 * D_HEAD), BF16),
        vmem((2, RANKS, HOME_LEN, 2 * D_HEAD), BF16),
        vmem((2, SLOTS, BLOCK, 2 * D_HEAD), BF16),
        pltpu.SMEM((POOL * RANKS,), jnp.int32),
        pltpu.SMEM((POOL * RANKS * MAXB,), jnp.int32),
        vmem((2, HEADS * D_HEAD, 2 * D_HEAD), BF16),
        vmem((RANKS, ROWS, D_HEAD), BF16),
        vmem((RANKS, MAXB, ROWS, D_HEAD), BF16),
        vmem((RANKS, HOME_AT + PART + ROWS, D_HEAD), BF16),
        vmem((RANKS, HOME_AT + PART + ROWS, D_HEAD), BF16),
        vmem((RANKS, ROWS, D_HEAD), BF16),
        vmem((CHIPS, RANKS, ROWS, D_HEAD), BF16),
        vmem((RANKS * CHIPS * ROWS, D_HEAD), F32),
        vmem((TP, 2, RANKS * 2 * KEPT, D_HEAD), BF16),
        vmem((TP * 2, RANKS * 2 * KEPT, D_HEAD), BF16),
        dma((5,)),
        dma((RANKS,)),
        dma,
        dma((2,)),
        dma,
        dma((RANKS,)),
        dma,
        dma((RANKS,)),
        dma,
        dma((2,)),
        dma((2,)),
    ]
    return pl.pallas_call(
        kernel,
        out_shape=pltpu.VMEM((POOL * RANKS // TP, STEPS, 2 * D_HEAD), BF16),
        in_specs=[pl.BlockSpec(memory_space=pl.ANY)] * len(args),
        out_specs=pl.BlockSpec(memory_space=pltpu.VMEM),
        scratch_shapes=scratch,
        compiler_params=pltpu.CompilerParams(
            collective_id=0, has_side_effects=True, vmem_limit_bytes=60 * 2**20
        ),
    )(*args)


def solution(mesh):
    return jax.shard_map(
        per_device,
        mesh=mesh,
        in_specs=(
            P("pool", None, "tp"),
            P("pool", None, "tp"),
            P("pool", None, "tp"),
            P("pool", None, "tp"),
            P("pool", None, "tp"),
            P("pool", None, "tp"),
            P("pool", None, "tp"),
            P(),
            P(),
            P("tp", "pool"),
        ),
        out_specs=P("tp", None, "pool"),
        check_vma=False,
    )
```
